256 devices in a mesh: grp: 4 (over x), seq: 16 (over z, core), tp: 4 (over y).
Axes of the slice: x: 4, y: 4, z: 8, core: 2. Of those that a mesh axis runs over, the one named last changes fastest.
Arguments:
- queries: bfloat16 [6144, 4096], P('seq', ('grp', 'tp')), may hold values from -5.5 to 5.5
- neighbour_states: bfloat16 [2, 96, 128, 4096], P(None, 'seq', None, ('grp', 'tp')), may hold values from -5.5 to 5.5
- retrieved: int32 [96, 2], P('seq'), may hold values from 0 to 95, as said below
- valid_blocks: int32 [96, 2], P('seq'), may hold values 0 or 1
- output_weight: bfloat16 [4096, 8192], P(('grp', 'tp')), may hold values from -0.75 to 0.75
- attention_cotangent: bfloat16 [6144, 4096], P('seq', ('grp', 'tp')), may hold values from -48 to 48
Outputs:
- layer_output: bfloat16 [6144, 8192], P('seq', ('grp', 'tp'))
- neighbour_gradient: bfloat16 [2, 96, 128, 4096], P(None, 'seq', None, ('grp', 'tp'))
The draws below stay inside these ranges and needn't reach their ends.
Inputs may be any that keep to these rules, and one draw needn't show every extreme that they name: `retrieved`: entries are store rows; row n is held by owner n // 6. Among the 12 entries of the spans of one index of seq, at most 2 name rows of one owner, and one owner, drawn from the seed, is named exactly 2 times by the spans of every index of seq.
All inputs are finite; a program needn't handle non-finite values. No bound on the sum of `valid_blocks` on one device may be relied on, other than what follows from the above.
Results may differ from the reference program's by a relative error of at most 0.019.
Values may be sent and summed in bfloat16 or wider, within the bound.
No kernel may reach another device: no remote copies, remote signals or barrier semaphores. Data moves between devices by JAX's collectives and lax.ppermute only.
A program may use at most 128 MiB of HBM per device.

```python
import jax
import jax.numpy as jnp
from jax import lax

D = 8192
HDIM = 128
SPAN = 64
NTOK = 128
KNB = 2
HD = 4096
REQ_DEV = 12
CAP = 2
NB_OWN = 6
SEQLEN = 6144
SPANS = 96
NBRS = 96
N_SEQ = 16


def draw_queries(key, part):
    key = jax.random.fold_in(key, 1)
    return jnp.clip(jax.random.normal(key, (SEQLEN, HD), jnp.float32), -5.5, 5.5).astype(jnp.bfloat16)


def draw_neighbour_states(key, part):
    key = jax.random.fold_in(key, 2)
    base_key = jax.random.fold_in(key, 0)
    full_shape = (2, NBRS, NTOK, HD)
    return jnp.clip(jax.random.normal(base_key, full_shape, jnp.float32), -5.5, 5.5).astype(jnp.bfloat16)


def draw_retrieved(key, part):
    key = jax.random.fold_in(key, 17)
    pick_key, popular_key, priority_key, mixing_key, row_key = jax.random.split(key, 5)
    common = jax.random.randint(pick_key, (), 0, N_SEQ)
    popularity = jax.random.randint(popular_key, (N_SEQ,), 0, 4)
    slot_count = N_SEQ * CAP
    labels = jnp.arange(slot_count, dtype=jnp.int32) // CAP
    raw_scores = jax.random.randint(priority_key, (N_SEQ, slot_count), 0, 4096)
    priority = raw_scores // (1 + popularity[labels])[None, :] + 1
    priority = jnp.where(labels[None, :] == common, 0, priority)
    priority = priority * slot_count + jnp.arange(slot_count)[None, :]
    ordering = jnp.argsort(priority, axis=1)
    chosen = labels[ordering[:, :REQ_DEV]]
    mixing = jax.random.randint(mixing_key, (N_SEQ, REQ_DEV), 0, 65536) * REQ_DEV + jnp.arange(REQ_DEV)[None, :]
    shuffle = jnp.argsort(mixing, axis=1)
    owners = jnp.take_along_axis(chosen, shuffle, axis=1)
    local_rows = jax.random.randint(row_key, (N_SEQ, REQ_DEV), 0, NB_OWN)
    return (owners * NB_OWN + local_rows).reshape(SPANS, KNB).astype(jnp.int32)


def place_ends(drawn, rng, least, high):
    longest = drawn.shape.index(max(drawn.shape))
    spots = []
    for shift in (0, 1):
        where = [jax.random.randint(jax.random.fold_in(rng, axis), (), 0, length) for axis, length in enumerate(drawn.shape)]
        where[longest] = (where[longest] + shift) % drawn.shape[longest]
        spots.append(tuple(where))
    return drawn.at[spots[0]].set(least).at[spots[1]].set(high)


def shard_levels(own_key, extent, cuts, least, largest):
    def one(axis_at, parts):
        draws = jax.random.uniform(jax.random.fold_in(jax.random.fold_in(own_key, 6), axis_at), (parts,), jnp.float32, least / len(cuts), largest / len(cuts))
        return jnp.repeat(jnp.exp(draws), extent[axis_at] // parts).reshape((-1,) + (1,) * (len(extent) - axis_at - 1))

    factor_of = one(*cuts[0])
    for cut in cuts[1:]:
        factor_of = factor_of * one(*cut)
    return factor_of


def scatter_about(key, extent, spread, reach, shards=(), held_as=jnp.bfloat16):
    gain = shard_levels(key, extent, shards, -0.22, 0.18) if shards else 1.0
    drawn = jax.random.normal(key, extent, jnp.float32) * spread * gain
    return jnp.minimum(jnp.maximum(drawn, -reach), reach).astype(held_as)


def setup_inputs(seed: int = 0) -> dict:
    key_of = jax.random.split(jax.random.key(seed), 7)
    return {
        "queries": draw_queries(jax.random.fold_in(key_of[6], 71), 0),
        "neighbour_states": draw_neighbour_states(jax.random.fold_in(key_of[6], 71), 0),
        "retrieved": draw_retrieved(jax.random.fold_in(key_of[6], 71), 0),
        "valid_blocks": place_ends((jax.random.randint(key_of[3], (SPANS, KNB), 0, 4) < 3).astype(jnp.int32), jax.random.fold_in(key_of[3], 1), 0, 1),
        "output_weight": scatter_about(key_of[4], (HD, D), (HD // 64) ** -0.5, 0.75, ((0, 16),)),
        "attention_cotangent": scatter_about(key_of[5], (SEQLEN, HD), 8.0, 48.0, ((0, 16), (1, 16))),
    }


def span_terms(query_rows, cotangent_rows, states, live_row):
    row_count, feature_count = query_rows.shape
    heads_here = feature_count // HDIM
    score_scale = HDIM ** -0.5
    query_heads = query_rows.astype(jnp.float32).reshape(row_count, heads_here, HDIM)
    cotangent_heads = cotangent_rows.astype(jnp.float32).reshape(row_count, heads_here, HDIM)
    key_heads = states[0].astype(jnp.float32).reshape(KNB * NTOK, heads_here, HDIM)
    value_heads = states[1].astype(jnp.float32).reshape(KNB * NTOK, heads_here, HDIM)
    live_keys = jnp.repeat(live_row, NTOK) > 0
    scores = jnp.einsum("qhd,khd->hqk", query_heads, key_heads) * score_scale
    masked = jnp.where(live_keys[None, None, :], scores, -1e30)
    row_max = jnp.max(masked, axis=-1, keepdims=True)
    unnormed = jnp.where(live_keys[None, None, :], jnp.exp(scores - row_max), 0.0)
    soft_weights = unnormed / jnp.maximum(jnp.sum(unnormed, axis=-1, keepdims=True), 1.0)
    rounded_weights = soft_weights.astype(jnp.bfloat16)
    attended = jnp.einsum("hqk,khd->qhd", rounded_weights.astype(jnp.float32), value_heads)
    attended = attended.astype(jnp.bfloat16).reshape(row_count, feature_count)
    weight_grads = jnp.einsum("qhd,khd->hqk", cotangent_heads, value_heads)
    row_delta = jnp.sum(soft_weights * weight_grads, axis=-1, keepdims=True)
    score_grads = (soft_weights * (weight_grads - row_delta)).astype(jnp.bfloat16)
    key_grad = jnp.einsum("hqk,qhd->khd", score_grads.astype(jnp.float32), query_heads) * score_scale
    value_grad = jnp.einsum("hqk,qhd->khd", rounded_weights.astype(jnp.float32), cotangent_heads)
    pair_grad = jnp.stack([key_grad, value_grad]).reshape(2, KNB, NTOK, feature_count)
    return attended, pair_grad.astype(jnp.bfloat16)


def reference(queries, neighbour_states, retrieved, valid_blocks, output_weight, attention_cotangent):
    lead_rows = SPAN - 1
    feature_count = queries.shape[1]
    query_tail = jnp.zeros((lead_rows, feature_count), queries.dtype)
    cotangent_tail = jnp.zeros((lead_rows, feature_count), attention_cotangent.dtype)
    shifted_queries = jnp.concatenate([queries[lead_rows:], query_tail]).reshape(SPANS, SPAN, feature_count)
    shifted_cotangent = jnp.concatenate([attention_cotangent[lead_rows:], cotangent_tail]).reshape(SPANS, SPAN, feature_count)

    def one_span(accumulator, operands):
        query_rows, cotangent_rows, ids_row, live_row = operands
        states = jnp.take(neighbour_states, ids_row.astype(jnp.int32), axis=1)
        attended, pair_grad = span_terms(query_rows, cotangent_rows, states, live_row)
        accumulator = accumulator.at[:, ids_row.astype(jnp.int32)].add(pair_grad.astype(jnp.float32))
        return accumulator, attended

    zero_sum = jnp.zeros(neighbour_states.shape, jnp.float32)
    summed, attended = lax.scan(one_span, zero_sum, (shifted_queries, shifted_cotangent, retrieved, valid_blocks))
    head_rows = jnp.zeros((lead_rows, feature_count), jnp.bfloat16)
    attention = jnp.concatenate([head_rows, attended.reshape(SEQLEN, feature_count)[:SEQLEN - lead_rows]])
    layer_output = jnp.dot(attention, output_weight, preferred_element_type=jnp.float32).astype(jnp.bfloat16)
    return (layer_output, summed.astype(jnp.bfloat16))
```

```python
import functools

import jax
import jax.numpy as jnp
from jax import lax
from jax.experimental import pallas as pl
from jax.experimental.pallas import tpu as pltpu
from jax.sharding import PartitionSpec as P

HDIM = 128
SPAN = 64
NTOK = 128
KNB = 2
CAP = 2
LEAD = SPAN - 1
FEATS = ("grp", "tp")
NT = (((1,), (1,)), ((), ()))
NN = (((1,), (0,)), ((), ()))
TN = (((0,), (0,)), ((), ()))
VMEM = pl.BlockSpec(memory_space=pltpu.VMEM)
SMEM = pl.BlockSpec(memory_space=pltpu.SMEM)
ANY = pl.BlockSpec(memory_space=pl.ANY)
LIMIT = pltpu.CompilerParams(vmem_limit_bytes=48 * 1024 * 1024)


def dot(a, b, dims):
    return lax.dot_general(a, b, dims, preferred_element_type=jnp.float32)


def three_parts(x):
    high = x.astype(jnp.bfloat16).astype(jnp.float32)
    middle = (x - high).astype(jnp.bfloat16).astype(jnp.float32)
    return [high, middle, x - high - middle]


def fill_window(rows_hbm, rows, sem):
    count = rows_hbm.shape[0]
    copy = pltpu.make_async_copy(rows_hbm, rows.at[pl.ds(0, count)], sem)
    copy.start()
    rows[pl.ds(count, SPAN), :] = jnp.zeros((SPAN, rows.shape[1]), rows.dtype)
    copy.wait()


def decode_slot(code):
    return code % 128, (code // 128) % 8, code // 1024


def pair_forward(slots, rows_hbm, states, out, rows, sem):
    fill_window(rows_hbm, rows, sem)
    width = states.shape[3]
    scale = HDIM ** (-0.5)

    def one_target(target, carry):
        stat_rows = []
        for place in range(CAP):
            span, row, _ = decode_slot(slots[target * CAP + place])
            tokens = rows[pl.ds(pl.multiple_of(span * SPAN, SPAN), 2 * SPAN), :]
            lse_heads, delta_heads, attended = [], [], []
            for at in range(0, width, HDIM):
                q = tokens[:, at : at + HDIM]
                g = tokens[:, width + at : width + at + HDIM]
                k = states[0, row, :, at : at + HDIM]
                v = states[1, row, :, at : at + HDIM]
                scores = dot(k, q, NT) * scale
                grads = dot(v, g, NT)
                top = jnp.max(scores, axis=0, keepdims=True)
                weights = jnp.exp(scores - top)
                total = jnp.sum(weights, axis=0, keepdims=True)
                weights = weights * (1.0 / total)
                lse_heads.append(top + jnp.log(total))
                delta_heads.append(jnp.sum(weights * grads, axis=0, keepdims=True))
                mixed = dot(weights.astype(jnp.bfloat16), v, TN)
                attended.append(mixed[LEAD : LEAD + SPAN])
            out[target, pl.ds(place * SPAN, SPAN), :] = jnp.concatenate(attended, 1).astype(out.dtype)
            stat_rows += three_parts(jnp.concatenate(lse_heads, 1))
            stat_rows += three_parts(jnp.concatenate(delta_heads, 1))
            stat_rows += [jnp.zeros((2, width), jnp.float32)]
        out[target, pl.ds(CAP * SPAN, 16), :] = jnp.concatenate(stat_rows, 0).astype(out.dtype)
        return carry

    lax.fori_loop(0, out.shape[0], one_target, 0)


def merge_pairs(requests, arrived, attention, stats):
    width = arrived.shape[2]
    for span in range(stats.shape[0]):
        lse, delta, live, parts = [], [], [], []
        for k in range(KNB):
            code = requests[span * KNB + k]
            owner, place, valid = code % 16, (code // 16) % 2, code // 32 > 0
            both = arrived[owner, pl.ds(CAP * SPAN, 16), :].astype(jnp.float32)
            mine = jnp.where(place == 0, both[0:8], both[8:16])
            lse.append(jnp.where(valid, mine[0:1] + (mine[1:2] + mine[2:3]), -1e30))
            delta.append(jnp.where(valid, mine[3:4] + (mine[4:5] + mine[5:6]), 0.0))
            live.append(valid)
            rows = arrived[owner, pl.ds(pl.multiple_of(place * SPAN, SPAN), SPAN), :]
            parts.append(jnp.where(valid, rows.astype(jnp.float32), 0.0))
        top = jnp.maximum(lse[0], lse[1])
        share = [jnp.where(live[k], jnp.exp(lse[k] - top), 0.0) for k in range(KNB)]
        total = jnp.maximum(share[0] + share[1], 1.0)
        share = [each / total for each in share]
        lse_all = top + jnp.log(total)
        delta_all = share[0] * delta[0] + share[1] * delta[1]
        heads = range(0, width, HDIM)
        stats[span] = jnp.concatenate(
            [lse_all[:, at : at + HDIM] for at in heads] + [delta_all[:, at : at + HDIM] for at in heads], 0
        )
        lines = [each[:, at : at + HDIM] for each in share for at in heads]
        square = jnp.concatenate(lines + [jnp.zeros((HDIM - len(lines), HDIM), jnp.float32)], 0).T
        columns = square[LEAD : LEAD + SPAN]
        count = len(heads)
        mixed = [
            parts[0][:, at : at + HDIM] * columns[:, h : h + 1]
            + parts[1][:, at : at + HDIM] * columns[:, count + h : count + h + 1]
            for h, at in enumerate(heads)
        ]
        attention[pl.ds(span * SPAN, SPAN), :] = jnp.concatenate(mixed, 1).astype(attention.dtype)


def pair_backward(slots, rows_hbm, states, stats, out, rows, total, sem):
    fill_window(rows_hbm, rows, sem)
    total[...] = jnp.zeros_like(total)
    width = states.shape[3]
    heads = width // HDIM
    scale = HDIM ** (-0.5)
    lane = lax.broadcasted_iota(jnp.int32, (NTOK, 2 * SPAN), 1)
    inside = (lane >= LEAD) & (lane < LEAD + SPAN)

    def one_target(target, carry):
        for place in range(CAP):
            span, row, live = decode_slot(slots[target * CAP + place])
            tokens = rows[pl.ds(pl.multiple_of(span * SPAN, SPAN), 2 * SPAN), :]
            lines = stats[span]
            seen = inside & (live > 0)
            for h in range(heads):
                at = h * HDIM
                q = tokens[:, at : at + HDIM]
                g = tokens[:, width + at : width + at + HDIM]
                k = states[0, row, :, at : at + HDIM]
                v = states[1, row, :, at : at + HDIM]
                scores = dot(k, q, NT) * scale
                weights = jnp.where(seen, jnp.exp(scores - lines[h : h + 1]), 0.0)
                grads = weights * (dot(v, g, NT) - lines[heads + h : heads + h + 1])
                total[0, row, :, at : at + HDIM] += dot(grads.astype(jnp.bfloat16), q, NN) * scale
                total[1, row, :, at : at + HDIM] += dot(weights.astype(jnp.bfloat16), g, NN)
        return carry

    lax.fori_loop(0, slots.shape[0] // CAP, one_target, 0)
    out[...] = total[...].astype(out.dtype)


def local(queries, neighbour_states, retrieved, valid_blocks, output_weight, attention_cotangent):
    owners = lax.axis_size("seq")
    me = lax.axis_index("seq")
    tok_rows, width = queries.shape
    span_count = tok_rows // SPAN
    request_count = span_count * KNB
    store_rows = neighbour_states.shape[1]

    gathered = lax.all_gather(
        jnp.concatenate([queries, attention_cotangent], axis=1), "seq", axis=0, tiled=True
    )
    weight_columns = lax.all_to_all(output_weight, FEATS, split_axis=1, concat_axis=0, tiled=True)
    table = lax.all_gather(
        jnp.stack([retrieved.reshape(request_count), valid_blocks.reshape(request_count)]), "seq", axis=0
    )
    owner_of = table[:, 0] // store_rows
    same_owner = owner_of[:, :, None] == owner_of[:, None, :]
    order = jnp.arange(request_count, dtype=jnp.int32)
    earlier = order[None, :] < order[:, None]
    position = jnp.sum((same_owner & earlier[None]).astype(jnp.int32), axis=2)
    span_of = jnp.arange(owners, dtype=jnp.int32)[:, None] * span_count + order[None, :] // KNB
    code = span_of + 128 * (table[:, 0] % store_rows) + 1024 * (table[:, 1] > 0).astype(jnp.int32)
    hit = (owner_of == me)[:, None, :] & (
        position[:, None, :] == jnp.arange(CAP, dtype=jnp.int32)[None, :, None]
    )
    slots = jnp.sum(jnp.where(hit, code[:, None, :], 0), axis=2).reshape(owners * CAP)
    mine = owner_of + 16 * position + 32 * (table[:, 1] > 0).astype(jnp.int32)
    requests = lax.dynamic_index_in_dim(mine, me, 0, keepdims=False)

    window = pltpu.VMEM((owners * tok_rows + SPAN, 2 * width), jnp.bfloat16)
    outgoing = pl.pallas_call(
        pair_forward,
        out_shape=jax.ShapeDtypeStruct((owners, CAP * SPAN + 16, width), jnp.bfloat16),
        in_specs=[SMEM, ANY, VMEM],
        out_specs=VMEM,
        scratch_shapes=[window, pltpu.SemaphoreType.DMA],
        compiler_params=LIMIT,
    )(slots, gathered, neighbour_states)
    arrived = lax.all_to_all(outgoing, "seq", split_axis=0, concat_axis=0, tiled=True)
    span_rows, stats = pl.pallas_call(
        merge_pairs,
        out_shape=(
            jax.ShapeDtypeStruct((tok_rows, width), jnp.bfloat16),
            jax.ShapeDtypeStruct((span_count, 2 * width // HDIM, HDIM), jnp.float32),
        ),
        in_specs=[SMEM, VMEM],
        out_specs=(VMEM, VMEM),
        compiler_params=LIMIT,
    )(requests, arrived)

    onward = [(source, source + 1) for source in range(owners - 1)]
    before = lax.ppermute(span_rows[tok_rows - SPAN :], "seq", onward)
    attention = jnp.concatenate([before[1:], span_rows[: tok_rows - LEAD]])
    all_heads = lax.all_gather(attention, FEATS, axis=1, tiled=True)
    layer_output = jnp.dot(all_heads, weight_columns, preferred_element_type=jnp.float32).astype(jnp.bfloat16)

    all_stats = lax.all_gather(stats, "seq", axis=0, tiled=True)
    neighbour_gradient = pl.pallas_call(
        pair_backward,
        out_shape=jax.ShapeDtypeStruct(neighbour_states.shape, jnp.bfloat16),
        in_specs=[SMEM, ANY, VMEM, VMEM],
        out_specs=VMEM,
        scratch_shapes=[
            window,
            pltpu.VMEM(neighbour_states.shape, jnp.float32),
            pltpu.SemaphoreType.DMA,
        ],
        compiler_params=LIMIT,
    )(slots, gathered, neighbour_states, all_stats)
    return (layer_output, neighbour_gradient)


def solution(mesh):
    placed = (
        P("seq", FEATS),
        P(None, "seq", None, FEATS),
        P("seq", None),
        P("seq", None),
        P(FEATS, None),
        P("seq", FEATS),
    )
    return jax.shard_map(
        local,
        mesh=mesh,
        in_specs=placed,
        out_specs=(P("seq", FEATS), P(None, "seq", None, FEATS)),
        check_vma=False,
    )
```

```python
import jax
import jax.numpy as jnp
from jax import lax
from jax.experimental import pallas as pl
from jax.experimental.pallas import tpu as pltpu
from jax.sharding import PartitionSpec as P

HDIM = 128
SPAN = 64
NTOK = 128
KNB = 2
CAP = 2
FEATS = ("grp", "tp")
NT = (((1,), (1,)), ((), ()))
NN = (((1,), (0,)), ((), ()))
TN = (((0,), (0,)), ((), ()))
VMEM = pl.BlockSpec(memory_space=pltpu.VMEM)
SMEM = pl.BlockSpec(memory_space=pltpu.SMEM)
ANY = pl.BlockSpec(memory_space=pl.ANY)
LIMIT = pltpu.CompilerParams(vmem_limit_bytes=48 * 1024 * 1024)


def cost(gigaflops):
    return pl.CostEstimate(flops=int(gigaflops * 1e9), bytes_accessed=8 * 1024 * 1024, transcendentals=0)


def dot(a, b, dims):
    return lax.dot_general(a, b, dims, preferred_element_type=jnp.float32)


def three_parts(x):
    high = x.astype(jnp.bfloat16).astype(jnp.float32)
    middle = (x - high).astype(jnp.bfloat16).astype(jnp.float32)
    return [high, middle, x - high - middle]


def decode_slot(code):
    return code % 128, (code // 128) % 8, code // 1024


def span_tokens(rows, span):
    block = jnp.minimum(span + 1, rows.shape[0] // SPAN - 1)
    main = rows[pl.ds(pl.multiple_of(block * SPAN, SPAN), SPAN), :]
    before = rows[pl.ds(pl.multiple_of(span * SPAN + SPAN - 16, 16), 16), :]
    place = lax.broadcasted_iota(jnp.int32, before.shape, 0)
    return jnp.concatenate([main[: SPAN - 16], jnp.where(place == 15, before, main[SPAN - 16 :])], 0)


def diagonal(first, second):
    zero = jnp.zeros_like(first)
    return jnp.concatenate(
        [jnp.concatenate([first, zero], 1), jnp.concatenate([zero, second], 1)], 0
    )


def pair_forward(slots, rows, states, out):
    width = states.shape[3]
    scale = HDIM ** (-0.5)

    def one_target(target, carry):
        span_0, row_0, _ = decode_slot(slots[target * CAP])
        span_1, row_1, _ = decode_slot(slots[target * CAP + 1])
        tokens_0, tokens_1 = span_tokens(rows, span_0), span_tokens(rows, span_1)
        lse_heads, delta_heads, attended_0, attended_1 = [], [], [], []
        for at in range(0, width, HDIM):
            q = diagonal(tokens_0[:, at : at + HDIM], tokens_1[:, at : at + HDIM])
            g = diagonal(
                tokens_0[:, width + at : width + at + HDIM], tokens_1[:, width + at : width + at + HDIM]
            )
            k = jnp.concatenate([states[0, row_0, :, at : at + HDIM], states[0, row_1, :, at : at + HDIM]], 1)
            v = jnp.concatenate([states[1, row_0, :, at : at + HDIM], states[1, row_1, :, at : at + HDIM]], 1)
            scores = dot(k, q, NT) * scale
            grads = dot(v, g, NT)
            top = jnp.max(scores, axis=0, keepdims=True)
            weights = jnp.exp(scores - top)
            total = jnp.sum(weights, axis=0, keepdims=True)
            weights = weights * (1.0 / total)
            lse_heads.append(top + jnp.log(total))
            delta_heads.append(jnp.sum(weights * grads, axis=0, keepdims=True))
            mixed = dot(weights.astype(jnp.bfloat16), v, TN)
            attended_0.append(mixed[:SPAN, :HDIM])
            attended_1.append(mixed[SPAN:, HDIM:])
        out[target, pl.ds(0, SPAN), :] = jnp.concatenate(attended_0, 1).astype(out.dtype)
        out[target, pl.ds(SPAN, SPAN), :] = jnp.concatenate(attended_1, 1).astype(out.dtype)
        lines = three_parts(jnp.concatenate(lse_heads, 1)) + three_parts(jnp.concatenate(delta_heads, 1))
        lines.append(jnp.zeros((16 - len(lines), width), jnp.float32))
        out[target, pl.ds(CAP * SPAN, 16), :] = jnp.concatenate(lines, 0).astype(out.dtype)
        return carry

    lax.fori_loop(0, out.shape[0], one_target, 0)


def merge_pairs(requests, arrived, *rest):
    attention, last, stats = rest[-3:]
    width = arrived.shape[2]
    heads = range(0, width, HDIM)
    count = len(heads)
    early = lax.broadcasted_iota(jnp.int32, (8, HDIM), 1) < SPAN
    final_row = lax.broadcasted_iota(jnp.int32, (SPAN, width), 0) == SPAN - 1
    previous = jnp.zeros((SPAN, width), jnp.float32)
    for span in range(stats.shape[0]):
        lse, delta, live, parts = [], [], [], []
        for k in range(KNB):
            code = requests[span * KNB + k]
            owner, place, valid = code % 16, (code // 16) % 2, code // 32 > 0
            both = arrived[owner, pl.ds(CAP * SPAN, 16), :].astype(jnp.float32)[:8]
            sides = []
            for at in heads:
                side = both[:, at : at + HDIM]
                sides.append(jnp.where(early == (place == 0), side, pltpu.roll(side, SPAN, 1)))
            mine = jnp.concatenate(sides, 1)
            lse.append(jnp.where(valid, mine[0:1] + (mine[1:2] + mine[2:3]), -1e30))
            delta.append(jnp.where(valid, mine[3:4] + (mine[4:5] + mine[5:6]), 0.0))
            live.append(valid)
            rows = arrived[owner, pl.ds(pl.multiple_of(place * SPAN, SPAN), SPAN), :]
            parts.append(jnp.where(valid, rows.astype(jnp.float32), 0.0))
        top = jnp.maximum(lse[0], lse[1])
        share = [jnp.where(live[k], jnp.exp(lse[k] - top), 0.0) for k in range(KNB)]
        total = jnp.maximum(share[0] + share[1], 1.0)
        share = [each / total for each in share]
        lse_all = top + jnp.log(total)
        delta_all = share[0] * delta[0] + share[1] * delta[1]
        stats[span] = jnp.concatenate(
            [lse_all[:, at : at + HDIM] for at in heads] + [delta_all[:, at : at + HDIM] for at in heads], 0
        )
        lines = [each[:, at : at + HDIM] for each in share for at in heads]
        columns = jnp.concatenate(lines + [jnp.zeros((HDIM - len(lines), HDIM), jnp.float32)], 0).T[:SPAN]
        mixed = jnp.concatenate(
            [
                parts[0][:, at : at + HDIM] * columns[:, h : h + 1]
                + parts[1][:, at : at + HDIM] * columns[:, count + h : count + h + 1]
                for h, at in enumerate(heads)
            ],
            1,
        )
        block = jnp.where(final_row, mixed, previous)
        attention[pl.ds(span * SPAN, SPAN), :] = block.astype(attention.dtype)
        previous = mixed
    last[...] = previous.astype(last.dtype)


def pair_backward(slots, rows, states, stats, out, total):
    total[...] = jnp.zeros_like(total)
    width = states.shape[3]
    heads = width // HDIM
    scale = HDIM ** (-0.5)
    lane = lax.broadcasted_iota(jnp.int32, (1, 2 * SPAN), 1)
    early = lane < SPAN
    first_token = lane % SPAN == SPAN - 1
    last_span = rows.shape[0] // SPAN - 1

    def one_target(target, carry):
        span_0, row_0, live_0 = decode_slot(slots[target * CAP])
        span_1, row_1, live_1 = decode_slot(slots[target * CAP + 1])
        tokens_0, tokens_1 = span_tokens(rows, span_0), span_tokens(rows, span_1)
        span = jnp.where(early, span_0, span_1)
        seen = (jnp.where(early, live_0, live_1) > 0) & (first_token | (span < last_span))
        lines = jnp.where(early, stats[span_0], stats[span_1])
        for h in range(heads):
            at = h * HDIM
            q = diagonal(tokens_0[:, at : at + HDIM], tokens_1[:, at : at + HDIM])
            g = diagonal(
                tokens_0[:, width + at : width + at + HDIM], tokens_1[:, width + at : width + at + HDIM]
            )
            k = jnp.concatenate([states[0, row_0, :, at : at + HDIM], states[0, row_1, :, at : at + HDIM]], 1)
            v = jnp.concatenate([states[1, row_0, :, at : at + HDIM], states[1, row_1, :, at : at + HDIM]], 1)
            scores = dot(k, q, NT) * scale
            weights = jnp.where(seen, jnp.exp(scores - lines[h : h + 1]), 0.0)
            grads = weights * (dot(v, g, NT) - lines[heads + h : heads + h + 1])
            key_part = dot(grads.astype(jnp.bfloat16), q, NN) * scale
            value_part = dot(weights.astype(jnp.bfloat16), g, NN)
            total[0, row_0, :, at : at + HDIM] += key_part[:, :HDIM]
            total[0, row_1, :, at : at + HDIM] += key_part[:, HDIM:]
            total[1, row_0, :, at : at + HDIM] += value_part[:, :HDIM]
            total[1, row_1, :, at : at + HDIM] += value_part[:, HDIM:]
        return carry

    lax.fori_loop(0, slots.shape[0] // CAP, one_target, 0)
    out[...] = total[...].astype(out.dtype)


def cut_weight(weight, *rest):
    pieces, sems = rest[:-1], rest[-1]
    grps, tps = lax.axis_size("grp"), lax.axis_size("tp")
    columns = pieces[0].shape[1]
    copies = []
    for i, piece in enumerate(pieces):
        g = lax.rem(lax.axis_index("grp") + i // tps, grps)
        t = lax.rem(lax.axis_index("tp") + i % tps, tps)
        start = pl.multiple_of((g * tps + t) * columns, 128)
        copies.append(pltpu.make_async_copy(weight.at[:, pl.ds(start, columns)], piece, sems.at[i]))
        copies[-1].start()
    for copy in copies:
        copy.wait()


def shifted(value, axis, steps):
    count = lax.axis_size(axis)
    return lax.ppermute(value, axis, [(source, (source + steps) % count) for source in range(count)])


def shifted_both(value, steps_grp, steps_tp):
    grps, tps = lax.axis_size("grp"), lax.axis_size("tp")
    pairs = [
        (g * tps + t, ((g + steps_grp) % grps) * tps + (t + steps_tp) % tps)
        for g in range(grps)
        for t in range(tps)
    ]
    return lax.ppermute(value, FEATS, pairs)


def halves_round(first, second, axis):
    half = first.shape[1] // 2
    count = lax.axis_size(axis)
    return [shifted(first[:, :half], axis, 1), shifted(second[:, half:], axis, count - 1)]


def project_near(*refs):
    blocks, weights, out = refs[:6], refs[6:-1], refs[-1]
    side = int(len(weights) ** 0.5)
    rows, width = blocks[0].shape[0], weights[0].shape[0]
    for half in range(2):
        total = None
        for block, step in zip(blocks[half * 3 : half * 3 + 3], (0, 1, side - 1)):
            for inner in range(side):
                weight = weights[inner * side + step] if half == 0 else weights[step * side + inner]
                term = dot(block[:, inner * width : (inner + 1) * width], weight[...], NN)
                total = term if total is None else total + term
        out[pl.ds(half * rows, rows), :] = total


def project_far(*refs):
    blocks, weights, partial, out = refs[:4], refs[4:-2], refs[-2], refs[-1]
    side = int(len(weights) ** 0.5)
    rows, width = blocks[0].shape[0], weights[0].shape[0]
    for half in range(2):
        total = partial[pl.ds(half * rows, rows), :]
        for inner in range(side):
            block = blocks[half * 2 + inner // (side // 2)]
            at = inner % (side // 2) * width
            weight = weights[inner * side + side // 2] if half == 0 else weights[side // 2 * side + inner]
            total = total + dot(block[:, at : at + width], weight[...], NN)
        out[pl.ds(half * rows, rows), :] = total.astype(out.dtype)


def local(queries, neighbour_states, retrieved, valid_blocks, output_weight, attention_cotangent):
    owners = lax.axis_size("seq")
    grps, tps = lax.axis_size("grp"), lax.axis_size("tp")
    me = lax.axis_index("seq")
    tok_rows, width = queries.shape
    span_count = tok_rows // SPAN
    request_count = span_count * KNB
    store_rows = neighbour_states.shape[1]
    out_columns = output_weight.shape[1] // (grps * tps)

    gathered = lax.all_gather(
        jnp.concatenate([queries, attention_cotangent], axis=1), "seq", axis=0, tiled=True
    )

    steps = [(dg, dt) for dg in range(grps) for dt in range(tps)]
    cut = pl.pallas_call(
        cut_weight,
        out_shape=[jax.ShapeDtypeStruct((width, out_columns), jnp.bfloat16)] * len(steps),
        in_specs=[ANY],
        out_specs=[ANY] * len(steps),
        scratch_shapes=[pltpu.SemaphoreType.DMA((len(steps),))],
    )(output_weight)
    weights = [shifted_both(piece, dg, dt) if dg or dt else piece for (dg, dt), piece in zip(steps, cut)]

    table = lax.all_gather(
        jnp.stack([retrieved.reshape(request_count), valid_blocks.reshape(request_count)]), "seq", axis=0
    )
    owner_of = table[:, 0] // store_rows
    same_owner = owner_of[:, :, None] == owner_of[:, None, :]
    order = jnp.arange(request_count, dtype=jnp.int32)
    earlier = order[None, :] < order[:, None]
    position = jnp.sum((same_owner & earlier[None]).astype(jnp.int32), axis=2)
    span_of = jnp.arange(owners, dtype=jnp.int32)[:, None] * span_count + order[None, :] // KNB
    code = span_of + 128 * (table[:, 0] % store_rows) + 1024 * (table[:, 1] > 0).astype(jnp.int32)
    hit = (owner_of == me)[:, None, :] & (
        position[:, None, :] == jnp.arange(CAP, dtype=jnp.int32)[None, :, None]
    )
    slots = jnp.sum(jnp.where(hit, code[:, None, :], 0), axis=2).reshape(owners * CAP)
    mine = owner_of + 16 * position + 32 * (table[:, 1] > 0).astype(jnp.int32)
    requests = lax.dynamic_index_in_dim(mine, me, 0, keepdims=False)

    outgoing = pl.pallas_call(
        pair_forward,
        cost_estimate=cost(9),
        out_shape=jax.ShapeDtypeStruct((owners, CAP * SPAN + 16, width), jnp.bfloat16),
        in_specs=[SMEM, VMEM, VMEM],
        out_specs=VMEM,
        compiler_params=LIMIT,
    )(slots, gathered, neighbour_states)
    arrived = lax.all_to_all(outgoing, "seq", split_axis=0, concat_axis=0, tiled=True)
    attention, last, stats = pl.pallas_call(
        merge_pairs,
        cost_estimate=cost(1),
        out_shape=(
            jax.ShapeDtypeStruct((tok_rows, width), jnp.bfloat16),
            jax.ShapeDtypeStruct((SPAN, width), jnp.bfloat16),
            jax.ShapeDtypeStruct((span_count, 2 * width // HDIM, HDIM), jnp.float32),
        ),
        in_specs=[SMEM, VMEM] + [ANY] * len(weights),
        out_specs=(VMEM, VMEM, VMEM),
        compiler_params=LIMIT,
    )(requests, arrived, *weights)

    middle = tok_rows // 2
    lower = attention[middle:]
    lower = jnp.concatenate([lower] + [shifted(lower, "tp", i) for i in range(1, tps)], 1)
    before = lax.ppermute(last, "seq", [(source, source + 1) for source in range(owners - 1)])
    final_row = lax.broadcasted_iota(jnp.int32, before.shape, 0) == SPAN - 1
    upper = jnp.concatenate([jnp.where(final_row, attention[:SPAN], before), attention[SPAN:middle]])
    upper = jnp.concatenate([upper] + [shifted(upper, "grp", i) for i in range(1, grps)], 1)
    upper = [upper, shifted(upper, "tp", 1), shifted(upper, "tp", tps - 1)]
    lower = [lower, shifted(lower, "grp", 1), shifted(lower, "grp", grps - 1)]
    far = halves_round(upper[1], upper[2], "tp") + halves_round(lower[1], lower[2], "grp")
    total = pl.pallas_call(
        project_near,
        cost_estimate=cost(3),
        out_shape=jax.ShapeDtypeStruct((tok_rows, out_columns), jnp.float32),
        in_specs=[VMEM] * (6 + len(weights)),
        out_specs=VMEM,
        compiler_params=LIMIT,
    )(*upper, *lower, *weights)
    layer_output = pl.pallas_call(
        project_far,
        cost_estimate=cost(2),
        out_shape=jax.ShapeDtypeStruct((tok_rows, out_columns), jnp.bfloat16),
        in_specs=[VMEM] * (5 + len(weights)),
        out_specs=VMEM,
        compiler_params=LIMIT,
    )(*far, *weights, total)

    all_stats = lax.all_gather(stats, "seq", axis=0, tiled=True)
    neighbour_gradient = pl.pallas_call(
        pair_backward,
        cost_estimate=cost(10),
        out_shape=jax.ShapeDtypeStruct(neighbour_states.shape, jnp.bfloat16),
        in_specs=[SMEM, VMEM, VMEM, VMEM],
        out_specs=VMEM,
        scratch_shapes=[pltpu.VMEM(neighbour_states.shape, jnp.float32)],
        compiler_params=LIMIT,
    )(slots, gathered, neighbour_states, all_stats)
    return (layer_output, neighbour_gradient)


def solution(mesh):
    placed = (
        P("seq", FEATS),
        P(None, "seq", None, FEATS),
        P("seq", None),
        P("seq", None),
        P(FEATS, None),
        P("seq", FEATS),
    )
    return jax.shard_map(
        local,
        mesh=mesh,
        in_specs=placed,
        out_specs=(P("seq", FEATS), P(None, "seq", None, FEATS)),
        check_vma=False,
    )
```

```python
import functools

import jax
import jax.numpy as jnp
from jax import lax
from jax.experimental import pallas as pl
from jax.experimental.pallas import tpu as pltpu
from jax.sharding import PartitionSpec as P

HDIM = 128
SPAN = 64
NTOK = 128
KNB = 2
CAP = 2
FEATS = ("grp", "tp")
LOG2E = 1.4426950408889634
NT = (((1,), (1,)), ((), ()))
NN = (((1,), (0,)), ((), ()))
TN = (((0,), (0,)), ((), ()))
VMEM = pl.BlockSpec(memory_space=pltpu.VMEM)
SMEM = pl.BlockSpec(memory_space=pltpu.SMEM)
ANY = pl.BlockSpec(memory_space=pl.ANY)
LIMIT = pltpu.CompilerParams(vmem_limit_bytes=48 * 1024 * 1024)


def cost(gigaflops):
    return pl.CostEstimate(flops=int(gigaflops * 1e9), bytes_accessed=8 * 1024 * 1024, transcendentals=0)


def dot(a, b, dims):
    return lax.dot_general(a, b, dims, preferred_element_type=jnp.float32)


def tied(value, *others):
    return pl.pallas_call(
        lambda *refs: None,
        out_shape=jax.ShapeDtypeStruct(value.shape, value.dtype),
        in_specs=[ANY] * (1 + len(others)),
        out_specs=ANY,
        input_output_aliases={0: 0},
    )(value, *others)


def decode_slot(code):
    return code & 127, (code >> 7) & 7, code >> 10


def span_tokens(rows, span):
    block = jnp.minimum(span + 1, rows.shape[0] // SPAN - 1)
    main = rows[pl.ds(pl.multiple_of(block * SPAN, SPAN), SPAN), :]
    before = rows[pl.ds(pl.multiple_of(span * SPAN + SPAN - 16, 16), 16), :]
    place = lax.broadcasted_iota(jnp.int32, before.shape, 0)
    return jnp.concatenate([main[: SPAN - 16], jnp.where(place == 15, before, main[SPAN - 16 :])], 0)


def diagonal(first, second):
    zero = jnp.zeros_like(first)
    return jnp.concatenate(
        [jnp.concatenate([first, zero], 1), jnp.concatenate([zero, second], 1)], 0
    )


def span_forward(codes, queries, cotangents, store, attention, stats, held, sems):
    blocks, width = queries.shape[0] // SPAN, queries.shape[1]
    windows = blocks + 1
    heads = range(0, width, HDIM)
    scale = HDIM ** (-0.5)
    copies = []
    for i in range(KNB * windows):
        row = codes[i] & 127
        source = store.at[lax.div(row, store.shape[2]), :, lax.rem(row, store.shape[2])]
        copies.append(pltpu.make_async_copy(source, held.at[i], sems.at[i]))
        copies[-1].start()

    lane = lax.broadcasted_iota(jnp.int32, (1, 2 * SPAN), 1)
    early = lane < SPAN
    place = lax.broadcasted_iota(jnp.int32, (16, width), 0)

    def window(ref, i):
        if i == 0 or i == blocks:
            at = min(i, blocks - 1) * SPAN
            return ref[at : at + SPAN, :]
        at = i * SPAN
        tail = jnp.where(place == 15, ref[at - 16 : at, :], ref[at + SPAN - 16 : at + SPAN, :])
        return jnp.concatenate([ref[at : at + SPAN - 16, :], tail], 0)

    attended, lines = {}, {}
    for first in range(0, windows, 2):
        second = min(first + 1, windows - 1)
        for i in range(KNB * first, KNB * (second + 1)):
            copies[i].wait()
        tokens = [window(queries, i) for i in (first, second)]
        others = [window(cotangents, i) for i in (first, second)]
        live = [jnp.where(early, codes[KNB * first + k] >> 7, codes[KNB * second + k] >> 7) > 0 for k in range(KNB)]
        for h, at in enumerate(heads):
            q = diagonal(*[each[:, at : at + HDIM] for each in tokens])
            g = diagonal(*[each[:, at : at + HDIM] for each in others])
            k, v = [
                jnp.concatenate(
                    [
                        jnp.concatenate([held[KNB * i + n, kind, :, at : at + HDIM] for n in range(KNB)], 0)
                        for i in (first, second)
                    ],
                    1,
                )
                for kind in range(2)
            ]
            scores = dot(k, q, NT)
            scores = [jnp.where(live[n], scores[n * NTOK : (n + 1) * NTOK], -1e30) for n in range(KNB)]
            top = jnp.max(jnp.maximum(scores[0], scores[1]), axis=0, keepdims=True)
            weights = [
                jnp.where(live[n], jnp.exp2((scores[n] - top) * (scale * LOG2E)), 0.0) for n in range(KNB)
            ]
            total = jnp.maximum(jnp.sum(weights[0] + weights[1], axis=0, keepdims=True), 1.0)
            weights = jnp.concatenate(weights, 0) * (1.0 / total)
            delta = jnp.sum(weights * dot(v, g, NT), axis=0, keepdims=True)
            mixed = dot(weights.astype(jnp.bfloat16), v, TN)
            attended[first, h], attended[second, h] = mixed[:SPAN, :HDIM], mixed[SPAN:, HDIM:]
            lines[first, h] = jnp.concatenate([top * scale + jnp.log(total), delta], 0)

    final_row = lax.broadcasted_iota(jnp.int32, (SPAN, width), 0) == SPAN - 1
    rolled = {key: pltpu.roll(jnp.concatenate([value] * 4, 0), SPAN, 1)[:2] for key, value in lines.items()}
    for i in range(blocks):
        mixed = [jnp.concatenate([attended[j, h] for h in range(len(heads))], 1) for j in (i, i + 1)]
        attention[pl.ds(i * SPAN, SPAN), :] = jnp.where(final_row, mixed[1], mixed[0]).astype(attention.dtype)
        rows = []
        for h in range(len(heads)):
            both = []
            for j in (i, i + 1):
                pair = (lines[j - j % 2, h], rolled[j - j % 2, h])
                both.append(jnp.where(early, pair[j % 2], pair[1 - j % 2]))
            rows.append(jnp.where(lane % SPAN == SPAN - 1, both[1], both[0]))
        stats[i] = jnp.concatenate([row[kind : kind + 1] for kind in range(2) for row in rows], 0)


def pair_backward(together, slots, rows, states, stats, out, total):
    total[...] = jnp.zeros_like(total)
    width = states.shape[3]
    heads = width // HDIM
    scale = HDIM ** (-0.5)
    lane = lax.broadcasted_iota(jnp.int32, (1, 2 * SPAN), 1)
    early = lane < SPAN
    first_token = lane % SPAN == SPAN - 1
    last_span = stats.shape[0] - 1

    def one_target(target):
        span_0, row_0, live_0 = decode_slot(slots[target * CAP])
        span_1, row_1, live_1 = decode_slot(slots[target * CAP + 1])
        tokens_0, tokens_1 = span_tokens(rows, span_0), span_tokens(rows, span_1)
        span = jnp.where(early, span_0, span_1)
        seen = (jnp.where(early, live_0, live_1) > 0) & (first_token | (span < last_span))
        lines = jnp.where(
            first_token,
            jnp.where(early, stats[span_0], stats[span_1]),
            jnp.where(
                early, stats[jnp.minimum(span_0 + 1, last_span)], stats[jnp.minimum(span_1 + 1, last_span)]
            ),
        )
        parts = []
        for h in range(heads):
            at = h * HDIM
            q = diagonal(tokens_0[:, at : at + HDIM], tokens_1[:, at : at + HDIM])
            g = diagonal(
                tokens_0[:, width + at : width + at + HDIM], tokens_1[:, width + at : width + at + HDIM]
            )
            k = jnp.concatenate([states[0, row_0, :, at : at + HDIM], states[0, row_1, :, at : at + HDIM]], 1)
            v = jnp.concatenate([states[1, row_0, :, at : at + HDIM], states[1, row_1, :, at : at + HDIM]], 1)
            scores = dot(k, q, NT) * scale
            weights = jnp.where(seen, jnp.exp(scores - lines[h : h + 1]), 0.0)
            grads = weights * (dot(v, g, NT) - lines[heads + h : heads + h + 1])
            key_part = dot(grads.astype(jnp.bfloat16), q, NN) * scale
            value_part = dot(weights.astype(jnp.bfloat16), g, NN)
            parts.append((key_part, value_part))
        return row_0, row_1, parts

    def some_targets(step, carry):
        results = [one_target(step * together + i) for i in range(together)]
        for row_0, row_1, parts in results:
            for h, pair in enumerate(parts):
                for kind, part in enumerate(pair):
                    total[kind, row_0, :, h * HDIM : (h + 1) * HDIM] += part[:, :HDIM]
                    total[kind, row_1, :, h * HDIM : (h + 1) * HDIM] += part[:, HDIM:]
        return carry

    lax.fori_loop(0, slots.shape[0] // CAP // together, some_targets, 0)
    out[...] = total[...].astype(out.dtype)


def cut_weight(core, columns, block):
    block[0] = columns[...]


def project(core, blocks, mine, other, out):
    columns = mine.shape[2]
    for weight, at in ((mine, core[0]), (other, 1 - core[0])):
        total = None
        for source in range(blocks.shape[0]):
            term = dot(blocks[source], weight[source], NN)
            total = term if total is None else total + term
        out[:, pl.ds(pl.multiple_of(at * columns, 128), columns)] = total.astype(out.dtype)


def local(queries, neighbour_states, retrieved, valid_blocks, output_weight, attention_cotangent):
    owners = lax.axis_size("seq")
    grps, tps = lax.axis_size("grp"), lax.axis_size("tp")
    me = lax.axis_index("seq")
    tok_rows, width = queries.shape
    span_count = tok_rows // SPAN
    request_count = span_count * KNB
    store_rows = neighbour_states.shape[1]
    out_columns = output_weight.shape[1] // (grps * tps)

    core = (me & 1).reshape(1)
    half = out_columns // 2
    cut = pl.pallas_call(
        cut_weight,
        grid_spec=pltpu.PrefetchScalarGridSpec(
            num_scalar_prefetch=1,
            grid=(grps * tps,),
            in_specs=[pl.BlockSpec((width, half), lambda i, core: (0, 2 * i + core[0]))],
            out_specs=pl.BlockSpec((1, width, half), lambda i, core: (i, 0, 0)),
        ),
        out_shape=jax.ShapeDtypeStruct((grps * tps, width, half), jnp.bfloat16),
    )(core, output_weight)
    weight = lax.all_to_all(cut, FEATS, split_axis=0, concat_axis=0, tiled=True)

    table = lax.all_gather(
        jnp.stack([retrieved.reshape(request_count), valid_blocks.reshape(request_count)]), "seq", axis=0
    )
    owner_of = table[:, 0] // store_rows
    same_owner = owner_of[:, :, None] == owner_of[:, None, :]
    order = jnp.arange(request_count, dtype=jnp.int32)
    earlier = order[None, :] < order[:, None]
    position = jnp.sum((same_owner & earlier[None]).astype(jnp.int32), axis=2)
    span_of = jnp.arange(owners, dtype=jnp.int32)[:, None] * span_count + order[None, :] // KNB
    code = span_of + 128 * (table[:, 0] % store_rows) + 1024 * (table[:, 1] > 0).astype(jnp.int32)
    hit = (owner_of == me)[:, None, :] & (
        position[:, None, :] == jnp.arange(CAP, dtype=jnp.int32)[None, :, None]
    )
    slots = jnp.sum(jnp.where(hit, code[:, None, :], 0), axis=2).reshape(owners * CAP)
    plain = (table[:, 0] + 128 * (table[:, 1] > 0).astype(jnp.int32)).reshape(owners * request_count)
    plain = jnp.concatenate([jnp.zeros((KNB,), jnp.int32), plain])
    codes = lax.dynamic_slice_in_dim(plain, me * request_count, request_count + KNB, 0)

    store = lax.all_gather(neighbour_states, "seq", axis=0)
    store = tied(store, slots, codes, weight)
    both = tied(jnp.concatenate([queries, attention_cotangent], axis=1), store)
    gathered = lax.all_gather(both, "seq", axis=0, tiled=True)
    weight_other = lax.ppermute(weight, "seq", [(source, source ^ 1) for source in range(owners)])

    attention, stats = pl.pallas_call(
        span_forward,
        cost_estimate=cost(5),
        out_shape=(
            jax.ShapeDtypeStruct((tok_rows, width), jnp.bfloat16),
            jax.ShapeDtypeStruct((span_count, 2 * width // HDIM, 2 * SPAN), jnp.float32),
        ),
        in_specs=[SMEM, VMEM, VMEM, ANY],
        out_specs=(VMEM, VMEM),
        scratch_shapes=[
            pltpu.VMEM((request_count + KNB, 2, NTOK, width), jnp.bfloat16),
            pltpu.SemaphoreType.DMA((request_count + KNB,)),
        ],
        compiler_params=LIMIT,
    )(codes, queries, attention_cotangent, store)

    spread = jnp.broadcast_to(attention[None], (grps * tps, tok_rows, width))
    heads = lax.all_to_all(spread, FEATS, split_axis=0, concat_axis=0, tiled=True)
    all_stats = lax.all_gather(stats, "seq", axis=0, tiled=True)
    neighbour_gradient = pl.pallas_call(
        functools.partial(pair_backward, 2),
        cost_estimate=cost(10),
        out_shape=jax.ShapeDtypeStruct(neighbour_states.shape, jnp.bfloat16),
        in_specs=[SMEM, VMEM, VMEM, VMEM],
        out_specs=VMEM,
        scratch_shapes=[pltpu.VMEM(neighbour_states.shape, jnp.float32)],
        compiler_params=LIMIT,
    )(slots, gathered, neighbour_states, all_stats)
    layer_output = pl.pallas_call(
        project,
        cost_estimate=cost(5),
        out_shape=jax.ShapeDtypeStruct((tok_rows, out_columns), jnp.bfloat16),
        in_specs=[SMEM, VMEM, VMEM, VMEM],
        out_specs=VMEM,
        compiler_params=LIMIT,
    )(core, heads, weight, weight_other)
    return (layer_output, neighbour_gradient)


def solution(mesh):
    placed = (
        P("seq", FEATS),
        P(None, "seq", None, FEATS),
        P("seq", None),
        P("seq", None),
        P(FEATS, None),
        P("seq", FEATS),
    )
    return jax.shard_map(
        local,
        mesh=mesh,
        in_specs=placed,
        out_specs=(P("seq", FEATS), P(None, "seq", None, FEATS)),
        check_vma=False,
    )
```

```python
import functools

import jax
import jax.numpy as jnp
from jax import lax
from jax.experimental import pallas as pl
from jax.experimental.pallas import tpu as pltpu
from jax.sharding import PartitionSpec as P

HDIM = 128
SPAN = 64
NTOK = 128
KNB = 2
CAP = 2
FEATS = ("grp", "tp")
LOG2E = 1.4426950408889634
NT = (((1,), (1,)), ((), ()))
NN = (((1,), (0,)), ((), ()))
TN = (((0,), (0,)), ((), ()))
VMEM = pl.BlockSpec(memory_space=pltpu.VMEM)
SMEM = pl.BlockSpec(memory_space=pltpu.SMEM)
ANY = pl.BlockSpec(memory_space=pl.ANY)
HBM = pl.BlockSpec(memory_space=pltpu.HBM)
LIMIT = pltpu.CompilerParams(vmem_limit_bytes=48 * 1024 * 1024)
WIDE = pltpu.CompilerParams(vmem_limit_bytes=60 * 1024 * 1024)


def cost(gigaflops):
    return pl.CostEstimate(flops=int(gigaflops * 1e9), bytes_accessed=8 * 1024 * 1024, transcendentals=0)


def dot(a, b, dims):
    return lax.dot_general(a, b, dims, preferred_element_type=jnp.float32)


def tied(value, *others):
    return pl.pallas_call(
        lambda *refs: None,
        out_shape=jax.ShapeDtypeStruct(value.shape, value.dtype),
        in_specs=[ANY] * (1 + len(others)),
        out_specs=ANY,
        input_output_aliases={0: 0},
    )(value, *others)


def decode_slot(code):
    return code & 127, (code >> 7) & 7, code >> 10


def span_tokens(window, span, spans):
    place = lax.broadcasted_iota(jnp.int32, (16, window.shape[1]), 0)
    first_token = (place == 15) & (span < spans - 1)
    tail = jnp.where(first_token, window[:16, :], window[SPAN:, :])
    return jnp.concatenate([window[16:SPAN, :], tail], 0)


def diagonal(first, second):
    zero = jnp.zeros_like(first)
    return jnp.concatenate(
        [jnp.concatenate([first, zero], 1), jnp.concatenate([zero, second], 1)], 0
    )


def span_forward(codes, queries, cotangents, store, spread, stats, held, attention, sems, out_sems):
    blocks, width = queries.shape[0] // SPAN, queries.shape[1]
    windows = blocks + 1
    heads = range(0, width, HDIM)
    scale = HDIM ** (-0.5)
    copies = []
    for i in range(KNB * windows):
        row = codes[i] & 127
        source = store.at[lax.div(row, store.shape[2]), :, lax.rem(row, store.shape[2])]
        copies.append(pltpu.make_async_copy(source, held.at[i], sems.at[i]))
        copies[-1].start()

    lane = lax.broadcasted_iota(jnp.int32, (1, 2 * SPAN), 1)
    early = lane < SPAN
    place = lax.broadcasted_iota(jnp.int32, (16, width), 0)

    def window(ref, i):
        if i == 0 or i == blocks:
            at = min(i, blocks - 1) * SPAN
            return ref[at : at + SPAN, :]
        at = i * SPAN
        tail = jnp.where(place == 15, ref[at - 16 : at, :], ref[at + SPAN - 16 : at + SPAN, :])
        return jnp.concatenate([ref[at : at + SPAN - 16, :], tail], 0)

    attended, lines = {}, {}
    for first in range(0, windows, 2):
        second = min(first + 1, windows - 1)
        for i in range(KNB * first, KNB * (second + 1)):
            copies[i].wait()
        tokens = [window(queries, i) for i in (first, second)]
        others = [window(cotangents, i) for i in (first, second)]
        live = [jnp.where(early, codes[KNB * first + k] >> 7, codes[KNB * second + k] >> 7) > 0 for k in range(KNB)]
        for h, at in enumerate(heads):
            q = diagonal(*[each[:, at : at + HDIM] for each in tokens])
            g = diagonal(*[each[:, at : at + HDIM] for each in others])
            k, v = [
                jnp.concatenate(
                    [
                        jnp.concatenate([held[KNB * i + n, kind, :, at : at + HDIM] for n in range(KNB)], 0)
                        for i in (first, second)
                    ],
                    1,
                )
                for kind in range(2)
            ]
            scores = dot(k, q, NT)
            scores = [jnp.where(live[n], scores[n * NTOK : (n + 1) * NTOK], -1e30) for n in range(KNB)]
            top = jnp.max(jnp.maximum(scores[0], scores[1]), axis=0, keepdims=True)
            weights = [
                jnp.where(live[n], jnp.exp2((scores[n] - top) * (scale * LOG2E)), 0.0) for n in range(KNB)
            ]
            total = jnp.maximum(jnp.sum(weights[0] + weights[1], axis=0, keepdims=True), 1.0)
            weights = jnp.concatenate(weights, 0) * (1.0 / total)
            delta = jnp.sum(weights * dot(v, g, NT), axis=0, keepdims=True)
            mixed = dot(weights.astype(jnp.bfloat16), v, TN)
            attended[first, h], attended[second, h] = mixed[:SPAN, :HDIM], mixed[SPAN:, HDIM:]
            lines[first, h] = jnp.concatenate([top * scale + jnp.log(total), delta], 0)

    final_row = lax.broadcasted_iota(jnp.int32, (SPAN, width), 0) == SPAN - 1
    rolled = {key: pltpu.roll(jnp.concatenate([value] * 4, 0), SPAN, 1)[:2] for key, value in lines.items()}
    for i in range(blocks):
        mixed = [jnp.concatenate([attended[j, h] for h in range(len(heads))], 1) for j in (i, i + 1)]
        attention[pl.ds(i * SPAN, SPAN), :] = jnp.where(final_row, mixed[1], mixed[0]).astype(attention.dtype)
        rows = []
        for h in range(len(heads)):
            both = []
            for j in (i, i + 1):
                pair = (lines[j - j % 2, h], rolled[j - j % 2, h])
                both.append(jnp.where(early, pair[j % 2], pair[1 - j % 2]))
            rows.append(jnp.where(lane % SPAN == SPAN - 1, both[1], both[0]))
        stats[i] = jnp.concatenate([row[kind : kind + 1] for kind in range(2) for row in rows], 0)
    copies = [pltpu.make_async_copy(attention, spread.at[i], out_sems.at[i]) for i in range(spread.shape[0])]
    for copy in copies:
        copy.start()
    for copy in copies:
        copy.wait()


def pair_backward(together, slots, rows, states, stats, out, finished, total, windows, sems):
    finished[...] = jnp.zeros_like(finished)
    spans = stats.shape[0]
    reach = SPAN + 16
    copies = []
    for i in range(slots.shape[0]):
        span = decode_slot(slots[i])[0]
        start = jnp.minimum(span * SPAN + SPAN - 16, rows.shape[0] - reach)
        source = rows.at[pl.ds(pl.multiple_of(start, 16), reach)]
        copies.append(pltpu.make_async_copy(source, windows.at[i], sems.at[i]))
        copies[-1].start()
    total[...] = jnp.zeros_like(total)
    width = states.shape[3]
    heads = width // HDIM
    scale = HDIM ** (-0.5)
    lane = lax.broadcasted_iota(jnp.int32, (1, 2 * SPAN), 1)
    early = lane < SPAN
    first_token = lane % SPAN == SPAN - 1
    last_span = stats.shape[0] - 1

    def one_target(target):
        span_0, row_0, live_0 = decode_slot(slots[target * CAP])
        span_1, row_1, live_1 = decode_slot(slots[target * CAP + 1])
        tokens_0 = span_tokens(windows.at[target * CAP], span_0, spans)
        tokens_1 = span_tokens(windows.at[target * CAP + 1], span_1, spans)
        span = jnp.where(early, span_0, span_1)
        seen = (jnp.where(early, live_0, live_1) > 0) & (first_token | (span < last_span))
        lines = jnp.where(
            first_token,
            jnp.where(early, stats[span_0], stats[span_1]),
            jnp.where(
                early, stats[jnp.minimum(span_0 + 1, last_span)], stats[jnp.minimum(span_1 + 1, last_span)]
            ),
        )
        parts = []
        for h in range(heads):
            at = h * HDIM
            q = diagonal(tokens_0[:, at : at + HDIM], tokens_1[:, at : at + HDIM])
            g = diagonal(
                tokens_0[:, width + at : width + at + HDIM], tokens_1[:, width + at : width + at + HDIM]
            )
            k = jnp.concatenate([states[0, row_0, :, at : at + HDIM], states[0, row_1, :, at : at + HDIM]], 1)
            v = jnp.concatenate([states[1, row_0, :, at : at + HDIM], states[1, row_1, :, at : at + HDIM]], 1)
            scores = dot(k, q, NT) * scale
            weights = jnp.where(seen, jnp.exp(scores - lines[h : h + 1]), 0.0)
            grads = weights * (dot(v, g, NT) - lines[heads + h : heads + h + 1])
            key_part = dot(grads.astype(jnp.bfloat16), q, NN) * scale
            value_part = dot(weights.astype(jnp.bfloat16), g, NN)
            parts.append((key_part, value_part))
        return row_0, row_1, parts

    def some_targets(step, carry):
        for i in range(together * CAP):
            at = step * together * CAP + i
            pltpu.make_async_copy(rows.at[pl.ds(0, reach)], windows.at[at], sems.at[at]).wait()
        results = [one_target(step * together + i) for i in range(together)]
        for row_0, row_1, parts in results:
            for h, pair in enumerate(parts):
                for kind, part in enumerate(pair):
                    total[kind, row_0, :, h * HDIM : (h + 1) * HDIM] += part[:, :HDIM]
                    total[kind, row_1, :, h * HDIM : (h + 1) * HDIM] += part[:, HDIM:]
        return carry

    lax.fori_loop(0, slots.shape[0] // CAP // together, some_targets, 0)
    out[...] = total[...].astype(out.dtype)


def cut_weight(core, columns, block):
    count, _, half = block.shape
    for i in range(count):
        at = pl.multiple_of((2 * i + core[0]) * half, 128)
        block[i] = columns[:, pl.ds(at, half)]


def project(core, blocks, mine, other, earlier, out, total):
    columns = mine.shape[2]
    step = pl.program_id(0)

    @pl.when(step == 0)
    def _():
        total[...] = jnp.zeros_like(total)

    for source in range(blocks.shape[0]):
        total[:, :columns] += dot(blocks[source], mine[source], NN)
        total[:, columns:] += dot(blocks[source], other[source], NN)

    @pl.when(step == pl.num_programs(0) - 1)
    def _():
        for weight, at in ((0, core[0]), (1, 1 - core[0])):
            part = total[:, weight * columns : (weight + 1) * columns]
            out[:, pl.ds(pl.multiple_of(at * columns, 128), columns)] = part.astype(out.dtype)


def local(queries, neighbour_states, retrieved, valid_blocks, output_weight, attention_cotangent):
    owners = lax.axis_size("seq")
    grps, tps = lax.axis_size("grp"), lax.axis_size("tp")
    me = lax.axis_index("seq")
    tok_rows, width = queries.shape
    span_count = tok_rows // SPAN
    request_count = span_count * KNB
    store_rows = neighbour_states.shape[1]
    out_columns = output_weight.shape[1] // (grps * tps)

    core = (me & 1).reshape(1)
    half = out_columns // 2
    sources = 4 if grps * tps % 4 == 0 else 1
    cut = pl.pallas_call(
        cut_weight,
        grid_spec=pltpu.PrefetchScalarGridSpec(
            num_scalar_prefetch=1,
            grid=(grps * tps // sources,),
            in_specs=[pl.BlockSpec((width, sources * out_columns), lambda i, core: (0, i))],
            out_specs=pl.BlockSpec((sources, width, half), lambda i, core: (i, 0, 0)),
        ),
        out_shape=jax.ShapeDtypeStruct((grps * tps, width, half), jnp.bfloat16),
    )(core, output_weight)
    weight = lax.all_to_all(cut, FEATS, split_axis=0, concat_axis=0, tiled=True)

    table = lax.all_gather(
        jnp.stack([retrieved.reshape(request_count), valid_blocks.reshape(request_count)]), "seq", axis=0
    )
    owner_of = table[:, 0] // store_rows
    same_owner = owner_of[:, :, None] == owner_of[:, None, :]
    order = jnp.arange(request_count, dtype=jnp.int32)
    earlier = order[None, :] < order[:, None]
    position = jnp.sum((same_owner & earlier[None]).astype(jnp.int32), axis=2)
    span_of = jnp.arange(owners, dtype=jnp.int32)[:, None] * span_count + order[None, :] // KNB
    code = span_of + 128 * (table[:, 0] % store_rows) + 1024 * (table[:, 1] > 0).astype(jnp.int32)
    hit = (owner_of == me)[:, None, :] & (
        position[:, None, :] == jnp.arange(CAP, dtype=jnp.int32)[None, :, None]
    )
    slots = jnp.sum(jnp.where(hit, code[:, None, :], 0), axis=2).reshape(owners * CAP)
    plain = (table[:, 0] + 128 * (table[:, 1] > 0).astype(jnp.int32)).reshape(owners * request_count)
    plain = jnp.concatenate([jnp.zeros((KNB,), jnp.int32), plain])
    codes = lax.dynamic_slice_in_dim(plain, me * request_count, request_count + KNB, 0)

    store = lax.all_gather(neighbour_states, "seq", axis=0)
    store = tied(store, slots, codes, weight)
    both = tied(jnp.concatenate([queries, attention_cotangent], axis=1), weight)
    gathered = lax.all_gather(both, "seq", axis=0, tiled=True)
    weight_other = lax.ppermute(weight, "seq", [(source, source ^ 1) for source in range(owners)])

    spread, stats = pl.pallas_call(
        span_forward,
        cost_estimate=cost(5),
        out_shape=(
            jax.ShapeDtypeStruct((grps * tps, tok_rows, width), jnp.bfloat16),
            jax.ShapeDtypeStruct((span_count, 2 * width // HDIM, 2 * SPAN), jnp.float32),
        ),
        in_specs=[SMEM, VMEM, VMEM, ANY],
        out_specs=(HBM, VMEM),
        scratch_shapes=[
            pltpu.VMEM((request_count + KNB, 2, NTOK, width), jnp.bfloat16),
            pltpu.VMEM((tok_rows, width), jnp.bfloat16),
            pltpu.SemaphoreType.DMA((request_count + KNB,)),
            pltpu.SemaphoreType.DMA((grps * tps,)),
        ],
        compiler_params=WIDE,
    )(codes, queries, attention_cotangent, store)

    heads = lax.all_to_all(spread, FEATS, split_axis=0, concat_axis=0, tiled=True)
    all_stats = lax.all_gather(stats, "seq", axis=0, tiled=True)
    neighbour_gradient, finished = pl.pallas_call(
        functools.partial(pair_backward, 4),
        cost_estimate=cost(10),
        out_shape=(
            jax.ShapeDtypeStruct(neighbour_states.shape, jnp.bfloat16),
            jax.ShapeDtypeStruct((8, HDIM), jnp.float32),
        ),
        in_specs=[SMEM, ANY, VMEM, VMEM],
        out_specs=(VMEM, VMEM),
        scratch_shapes=[
            pltpu.VMEM(neighbour_states.shape, jnp.float32),
            pltpu.VMEM((owners * CAP, SPAN + 16, 2 * width), jnp.bfloat16),
            pltpu.SemaphoreType.DMA((owners * CAP,)),
        ],
        compiler_params=LIMIT,
    )(slots, gathered, neighbour_states, all_stats)
    layer_output = pl.pallas_call(
        project,
        cost_estimate=cost(5),
        grid_spec=pltpu.PrefetchScalarGridSpec(
            num_scalar_prefetch=1,
            grid=(grps * tps // sources,),
            in_specs=[
                pl.BlockSpec((sources, tok_rows, width), lambda i, core: (i, 0, 0)),
                pl.BlockSpec((sources, width, half), lambda i, core: (i, 0, 0)),
                pl.BlockSpec((sources, width, half), lambda i, core: (i, 0, 0)),
                ANY,
            ],
            out_specs=pl.BlockSpec((tok_rows, out_columns), lambda i, core: (0, 0)),
            scratch_shapes=[pltpu.VMEM((tok_rows, out_columns), jnp.float32)],
        ),
        out_shape=jax.ShapeDtypeStruct((tok_rows, out_columns), jnp.bfloat16),
        compiler_params=LIMIT,
    )(core, heads, weight, weight_other, finished)
    return (layer_output, neighbour_gradient)


def solution(mesh):
    placed = (
        P("seq", FEATS),
        P(None, "seq", None, FEATS),
        P("seq", None),
        P("seq", None),
        P(FEATS, None),
        P("seq", FEATS),
    )
    return jax.shard_map(
        local,
        mesh=mesh,
        in_specs=placed,
        out_specs=(P("seq", FEATS), P(None, "seq", None, FEATS)),
        check_vma=False,
    )
```

```python
import functools

import jax
import jax.numpy as jnp
from jax import lax
from jax.experimental import pallas as pl
from jax.experimental.pallas import tpu as pltpu
from jax.sharding import PartitionSpec as P

HDIM = 128
SPAN = 64
NTOK = 128
KNB = 2
CAP = 2
FEATS = ("grp", "tp")
LOG2E = 1.4426950408889634
NT = (((1,), (1,)), ((), ()))
NN = (((1,), (0,)), ((), ()))
TN = (((0,), (0,)), ((), ()))
VMEM = pl.BlockSpec(memory_space=pltpu.VMEM)
SMEM = pl.BlockSpec(memory_space=pltpu.SMEM)
ANY = pl.BlockSpec(memory_space=pl.ANY)
LIMIT = pltpu.CompilerParams(vmem_limit_bytes=48 * 1024 * 1024)
WIDE = pltpu.CompilerParams(vmem_limit_bytes=60 * 1024 * 1024)


def cost(gigaflops):
    return pl.CostEstimate(flops=int(gigaflops * 1e9), bytes_accessed=8 * 1024 * 1024, transcendentals=0)


def dot(a, b, dims):
    return lax.dot_general(a, b, dims, preferred_element_type=jnp.float32)


def tied(value, *others):
    return pl.pallas_call(
        lambda *refs: None,
        out_shape=jax.ShapeDtypeStruct(value.shape, value.dtype),
        in_specs=[ANY] * (1 + len(others)),
        out_specs=ANY,
        input_output_aliases={0: 0},
    )(value, *others)


def three_parts(x):
    high = x.astype(jnp.bfloat16).astype(jnp.float32)
    middle = (x - high).astype(jnp.bfloat16).astype(jnp.float32)
    return [high, middle, x - high - middle]


def decode_slot(code):
    return code & 127, (code >> 7) & 7, code >> 10


def span_tokens(window, span, spans):
    place = lax.broadcasted_iota(jnp.int32, (16, window.shape[1]), 0)
    first_token = (place == 15) & (span < spans - 1)
    tail = jnp.where(first_token, window[:16, :], window[SPAN:, :])
    return jnp.concatenate([window[16:SPAN, :], tail], 0)


def diagonal(first, second):
    zero = jnp.zeros_like(first)
    return jnp.concatenate(
        [jnp.concatenate([first, zero], 1), jnp.concatenate([zero, second], 1)], 0
    )


def whole_tokens(rows, span):
    block = jnp.minimum(span + 1, rows.shape[0] // SPAN - 1)
    main = rows[pl.ds(pl.multiple_of(block * SPAN, SPAN), SPAN), :]
    before = rows[pl.ds(pl.multiple_of(span * SPAN + SPAN - 16, 16), 16), :]
    place = lax.broadcasted_iota(jnp.int32, before.shape, 0)
    return jnp.concatenate([main[: SPAN - 16], jnp.where(place == 15, before, main[SPAN - 16 :])], 0)


def pair_forward(together, distances, slots, states, *rest):
    pieces, (out, rows, sems) = rest[:-3], rest[-3:]
    per_core = len(pieces) // 2
    me = lax.axis_index("seq")
    chips = lax.axis_size("seq") // 2
    height = rows.shape[0] // (2 * chips)
    copies = []
    for i, piece in enumerate(pieces):
        distance, start = distances[i % per_core]
        chip = lax.rem(lax.div(me, 2) + (chips - distance) % chips, chips)
        core = lax.rem(lax.rem(me, 2) + i // per_core, 2)
        at = pl.multiple_of((chip * 2 + core) * height + start, 64)
        copies.append(pltpu.make_async_copy(piece, rows.at[pl.ds(at, piece.shape[0])], sems.at[i]))
        copies[-1].start()
    for copy in copies:
        copy.wait()
    width = states.shape[3]
    scale = HDIM ** (-0.5)

    def one_target(target):
        span_0, row_0, _ = decode_slot(slots[target * CAP])
        span_1, row_1, _ = decode_slot(slots[target * CAP + 1])
        tokens_0, tokens_1 = whole_tokens(rows, span_0), whole_tokens(rows, span_1)
        lse_heads, attended_0, attended_1 = [], [], []
        for at in range(0, width, HDIM):
            q = diagonal(tokens_0[:, at : at + HDIM], tokens_1[:, at : at + HDIM])
            k = jnp.concatenate([states[0, row_0, :, at : at + HDIM], states[0, row_1, :, at : at + HDIM]], 1)
            v = jnp.concatenate([states[1, row_0, :, at : at + HDIM], states[1, row_1, :, at : at + HDIM]], 1)
            scores = dot(k, q, NT)
            top = jnp.max(scores, axis=0, keepdims=True)
            weights = jnp.exp2((scores - top) * (scale * LOG2E))
            total = jnp.sum(weights, axis=0, keepdims=True)
            weights = weights * (1.0 / total)
            lse_heads.append(top * scale + jnp.log(total))
            mixed = dot(weights.astype(jnp.bfloat16), v, TN)
            attended_0.append(mixed[:SPAN, :HDIM])
            attended_1.append(mixed[SPAN:, HDIM:])
        lines = three_parts(jnp.concatenate(lse_heads, 1))
        lines.append(jnp.zeros((16 - len(lines), width), jnp.float32))
        return [jnp.concatenate(each, 1) for each in (attended_0, attended_1)] + [jnp.concatenate(lines, 0)]

    def some_targets(step, carry):
        results = [one_target(step * together + i) for i in range(together)]
        for i, parts in enumerate(results):
            target = step * together + i
            out[target, pl.ds(0, SPAN), :] = parts[0].astype(out.dtype)
            out[target, pl.ds(SPAN, SPAN), :] = parts[1].astype(out.dtype)
            out[target, pl.ds(CAP * SPAN, 16), :] = parts[2].astype(out.dtype)
        return carry

    lax.fori_loop(0, out.shape[0] // together, some_targets, 0)


def merge_pairs(requests, arrived, cotangents, next_block, *rest):
    upper, lower, last, stats = rest[-4:]
    width = arrived.shape[2]
    heads = range(0, width, HDIM)
    count = len(heads)
    spans = stats.shape[0]
    early = lax.broadcasted_iota(jnp.int32, (8, HDIM), 1) < SPAN
    lane = lax.broadcasted_iota(jnp.int32, (SPAN, HDIM), 1)
    place = lax.broadcasted_iota(jnp.int32, (16, width), 0)
    final_row = lax.broadcasted_iota(jnp.int32, (SPAN, width), 0) == SPAN - 1
    previous = jnp.zeros((SPAN, width), jnp.float32)
    for span in range(spans):
        lse, live, parts = [], [], []
        for k in range(KNB):
            code = requests[span * KNB + k]
            owner, side, valid = code & 15, (code >> 4) & 1, code >> 5 > 0
            both = arrived[owner, pl.ds(CAP * SPAN, 16), :].astype(jnp.float32)[:8]
            sides = []
            for at in heads:
                part = both[:, at : at + HDIM]
                sides.append(jnp.where(early == (side == 0), part, pltpu.roll(part, SPAN, 1)))
            mine = jnp.concatenate(sides, 1)
            lse.append(jnp.where(valid, mine[0:1] + (mine[1:2] + mine[2:3]), -1e30))
            live.append(valid)
            rows = arrived[owner, pl.ds(pl.multiple_of(side * SPAN, SPAN), SPAN), :]
            parts.append(jnp.where(valid, rows.astype(jnp.float32), 0.0))
        top = jnp.maximum(lse[0], lse[1])
        share = [jnp.where(live[k], jnp.exp(lse[k] - top), 0.0) for k in range(KNB)]
        total = jnp.maximum(share[0] + share[1], 1.0)
        share = [each / total for each in share]
        lse_all = top + jnp.log(total)
        lines = [each[:, at : at + HDIM] for each in share for at in heads]
        columns = jnp.concatenate(lines + [jnp.zeros((HDIM - len(lines), HDIM), jnp.float32)], 0).T[:SPAN]
        mixed = jnp.concatenate(
            [
                parts[0][:, at : at + HDIM] * columns[:, h : h + 1]
                + parts[1][:, at : at + HDIM] * columns[:, count + h : count + h + 1]
                for h, at in enumerate(heads)
            ],
            1,
        )
        block = jnp.where(final_row, mixed, previous)
        half, place_in = (upper, span) if span < spans // 2 else (lower, span - spans // 2)
        half[pl.ds(place_in * SPAN, SPAN), :] = block.astype(half.dtype)
        previous = mixed
        main = cotangents[(span + 1) * SPAN : (span + 2) * SPAN, :] if span < spans - 1 else next_block[...]
        before = cotangents[(span + 1) * SPAN - 16 : (span + 1) * SPAN, :]
        tail = jnp.where(place == 15, before, main[SPAN - 16 :])
        product = mixed * jnp.concatenate([main[: SPAN - 16], tail], 0).astype(jnp.float32)
        square = jnp.zeros((SPAN, HDIM), jnp.float32)
        for h, at in enumerate(heads):
            square = jnp.where(lane == h, jnp.sum(product[:, at : at + HDIM], axis=1, keepdims=True), square)
        delta = jnp.concatenate([square, square], 0).T[:count]
        stats[span] = jnp.concatenate([lse_all[:, at : at + HDIM] for at in heads] + [delta], 0)
    last[...] = previous.astype(last.dtype)


def pair_backward(together, slots, queries, cotangents, states, stats, out, finished, total, windows, sems):
    finished[...] = jnp.zeros_like(finished)
    spans = stats.shape[0]
    reach = SPAN + 16
    for i in range(slots.shape[0]):
        span = decode_slot(slots[i])[0]
        start = jnp.minimum(span * SPAN + SPAN - 16, queries.shape[0] - reach)
        for kind, rows in enumerate((queries, cotangents)):
            source = rows.at[pl.ds(pl.multiple_of(start, 16), reach)]
            pltpu.make_async_copy(source, windows.at[kind, i], sems.at[kind, i]).start()
    total[...] = jnp.zeros_like(total)
    width = states.shape[3]
    heads = width // HDIM
    scale = HDIM ** (-0.5)
    lane = lax.broadcasted_iota(jnp.int32, (1, 2 * SPAN), 1)
    early = lane < SPAN
    first_token = lane % SPAN == SPAN - 1
    last_span = stats.shape[0] - 1

    def one_target(target):
        span_0, row_0, live_0 = decode_slot(slots[target * CAP])
        span_1, row_1, live_1 = decode_slot(slots[target * CAP + 1])
        q_0, g_0 = [span_tokens(windows.at[kind, target * CAP], span_0, spans) for kind in range(2)]
        q_1, g_1 = [span_tokens(windows.at[kind, target * CAP + 1], span_1, spans) for kind in range(2)]
        span = jnp.where(early, span_0, span_1)
        seen = (jnp.where(early, live_0, live_1) > 0) & (first_token | (span < last_span))
        lines = jnp.where(early, stats[span_0], stats[span_1])
        parts = []
        for h in range(heads):
            at = h * HDIM
            q = diagonal(q_0[:, at : at + HDIM], q_1[:, at : at + HDIM])
            g = diagonal(g_0[:, at : at + HDIM], g_1[:, at : at + HDIM])
            k = jnp.concatenate([states[0, row_0, :, at : at + HDIM], states[0, row_1, :, at : at + HDIM]], 1)
            v = jnp.concatenate([states[1, row_0, :, at : at + HDIM], states[1, row_1, :, at : at + HDIM]], 1)
            scores = dot(k, q, NT) * scale
            weights = jnp.where(seen, jnp.exp(scores - lines[h : h + 1]), 0.0)
            grads = weights * (dot(v, g, NT) - lines[heads + h : heads + h + 1])
            key_part = dot(grads.astype(jnp.bfloat16), q, NN) * scale
            value_part = dot(weights.astype(jnp.bfloat16), g, NN)
            parts.append((key_part, value_part))
        return row_0, row_1, parts

    def some_targets(step, carry):
        for i in range(together * CAP):
            at = step * together * CAP + i
            for kind, rows in enumerate((queries, cotangents)):
                pltpu.make_async_copy(
                    rows.at[pl.ds(0, reach)], windows.at[kind, at], sems.at[kind, at]
                ).wait()
        results = [one_target(step * together + i) for i in range(together)]
        for row_0, row_1, parts in results:
            for h, pair in enumerate(parts):
                for kind, part in enumerate(pair):
                    total[kind, row_0, :, h * HDIM : (h + 1) * HDIM] += part[:, :HDIM]
                    total[kind, row_1, :, h * HDIM : (h + 1) * HDIM] += part[:, HDIM:]
        return carry

    lax.fori_loop(0, slots.shape[0] // CAP // together, some_targets, 0)
    out[...] = total[...].astype(out.dtype)


def cut_weight(core, columns, block):
    count, _, half = block.shape
    for i in range(count):
        at = pl.multiple_of((2 * i + core[0]) * half, 128)
        block[i] = columns[:, pl.ds(at, half)]


def shifted(value, axis, steps):
    count = lax.axis_size(axis)
    return lax.ppermute(value, axis, [(source, (source + steps) % count) for source in range(count)])


def halves_round(first, second, axis):
    half = first.shape[1] // 2
    return [shifted(first[:, :half], axis, 1), shifted(second[:, half:], axis, lax.axis_size(axis) - 1)]


def source_of(steps_grp, steps_tp):
    grps, tps = lax.axis_size("grp"), lax.axis_size("tp")
    grp = lax.rem(lax.axis_index("grp") + (grps - steps_grp) % grps, grps)
    return grp * tps + lax.rem(lax.axis_index("tp") + (tps - steps_tp) % tps, tps)


def project_near(*refs):
    blocks, weights, out = refs[:6], refs[6:8], refs[-1]
    side = lax.axis_size("tp")
    rows, width = blocks[0].shape[0], weights[0].shape[1]
    for half in range(2):
        for kind, weight in enumerate(weights):
            total = None
            for block, step in zip(blocks[half * 3 : half * 3 + 3], (0, 1, side - 1)):
                for inner in range(side):
                    source = source_of(inner, step) if half == 0 else source_of(step, inner)
                    term = dot(block[:, inner * width : (inner + 1) * width], weight[source], NN)
                    total = term if total is None else total + term
            out[kind, pl.ds(half * rows, rows), :] = total


def project_far(*refs):
    blocks, weights, partial, out = refs[:4], refs[4:6], refs[6], refs[7]
    side = lax.axis_size("tp")
    rows, width = blocks[0].shape[0], weights[0].shape[1]
    columns = weights[0].shape[2]
    core = lax.rem(lax.axis_index("seq"), 2)
    for half in range(2):
        for kind, weight in enumerate(weights):
            total = partial[kind, pl.ds(half * rows, rows), :]
            for inner in range(side):
                block = blocks[half * 2 + inner // (side // 2)]
                at = inner % (side // 2) * width
                far = side // 2
                source = source_of(inner, far) if half == 0 else source_of(far, inner)
                total = total + dot(block[:, at : at + width], weight[source], NN)
            at = pl.multiple_of((core if kind == 0 else 1 - core) * columns, 128)
            out[pl.ds(half * rows, rows), pl.ds(at, columns)] = total.astype(out.dtype)


def local(queries, neighbour_states, retrieved, valid_blocks, output_weight, attention_cotangent):
    owners = lax.axis_size("seq")
    grps, tps = lax.axis_size("grp"), lax.axis_size("tp")
    me = lax.axis_index("seq")
    tok_rows, width = queries.shape
    span_count = tok_rows // SPAN
    request_count = span_count * KNB
    store_rows = neighbour_states.shape[1]
    out_columns = output_weight.shape[1] // (grps * tps)

    core = (me & 1).reshape(1)
    half = out_columns // 2
    sources = 4 if grps * tps % 4 == 0 else 1
    cut = pl.pallas_call(
        cut_weight,
        grid_spec=pltpu.PrefetchScalarGridSpec(
            num_scalar_prefetch=1,
            grid=(grps * tps // sources,),
            in_specs=[pl.BlockSpec((width, sources * out_columns), lambda i, core: (0, i))],
            out_specs=pl.BlockSpec((sources, width, half), lambda i, core: (i, 0, 0)),
        ),
        out_shape=jax.ShapeDtypeStruct((grps * tps, width, half), jnp.bfloat16),
    )(core, output_weight)
    weight = lax.all_to_all(cut, FEATS, split_axis=0, concat_axis=0, tiled=True)

    table = jnp.stack([retrieved.reshape(request_count), valid_blocks.reshape(request_count)])[None]
    distance = 1
    while distance < owners:
        there = lax.ppermute(table, "seq", [(at, at ^ distance) for at in range(owners)])
        table = jnp.where(
            (me & distance) > 0, jnp.concatenate([there, table]), jnp.concatenate([table, there])
        )
        distance *= 2
    owner_of = table[:, 0] // store_rows
    same_owner = owner_of[:, :, None] == owner_of[:, None, :]
    order = jnp.arange(request_count, dtype=jnp.int32)
    earlier = order[None, :] < order[:, None]
    position = jnp.sum((same_owner & earlier[None]).astype(jnp.int32), axis=2)
    span_of = jnp.arange(owners, dtype=jnp.int32)[:, None] * span_count + order[None, :] // KNB
    code = span_of + 128 * (table[:, 0] % store_rows) + 1024 * (table[:, 1] > 0).astype(jnp.int32)
    hit = (owner_of == me)[:, None, :] & (
        position[:, None, :] == jnp.arange(CAP, dtype=jnp.int32)[None, :, None]
    )
    slots = jnp.sum(jnp.where(hit, code[:, None, :], 0), axis=2).reshape(owners * CAP)
    mine = owner_of + 16 * position + 32 * (table[:, 1] > 0).astype(jnp.int32)
    requests = lax.dynamic_index_in_dim(mine, me, 0, keepdims=False)

    def steps(value, chips):
        return lax.ppermute(value, "seq", [(at, (at + 2 * chips) % owners) for at in range(owners)])

    def swap(value):
        return lax.ppermute(value, "seq", [(at, at ^ 1) for at in range(owners)])

    middle = tok_rows // 2
    up_1, down_1, up_2, down_2 = [steps(queries, i) for i in (1, -1, 2, -2)]
    far = [steps(up_2, 1), steps(down_2, -1), steps(up_2[:middle], 2), steps(down_2[middle:], -2)]
    distances = [(0, 0), (1, 0), (-1, 0), (2, 0), (-2, 0), (3, 0), (-3, 0), (4, 0), (4, middle)]
    pieces = [queries, up_1, down_1, up_2, down_2, *far]
    pieces = pieces + [swap(piece) for piece in pieces]
    next_block = lax.ppermute(attention_cotangent[:SPAN], "seq", [(at + 1, at) for at in range(owners - 1)])
    cotangents = lax.all_gather(attention_cotangent, "seq", axis=0, tiled=True)

    outgoing, all_queries = pl.pallas_call(
        functools.partial(pair_forward, 2, distances),
        cost_estimate=cost(8),
        out_shape=(
            jax.ShapeDtypeStruct((owners, CAP * SPAN + 16, width), jnp.bfloat16),
            jax.ShapeDtypeStruct((owners * tok_rows, width), jnp.bfloat16),
        ),
        in_specs=[SMEM, VMEM] + [ANY] * len(pieces),
        out_specs=(VMEM, VMEM),
        scratch_shapes=[pltpu.SemaphoreType.DMA((len(pieces),))],
        compiler_params=LIMIT,
    )(slots, neighbour_states, *pieces)
    arrived = lax.all_to_all(outgoing, "seq", split_axis=0, concat_axis=0, tiled=True)
    upper, lower, last, stats = pl.pallas_call(
        merge_pairs,
        cost_estimate=cost(2),
        out_shape=(
            jax.ShapeDtypeStruct((middle, width), jnp.bfloat16),
            jax.ShapeDtypeStruct((middle, width), jnp.bfloat16),
            jax.ShapeDtypeStruct((SPAN, width), jnp.bfloat16),
            jax.ShapeDtypeStruct((span_count, 2 * width // HDIM, 2 * SPAN), jnp.float32),
        ),
        in_specs=[SMEM, VMEM, VMEM, VMEM, ANY],
        out_specs=(VMEM, VMEM, VMEM, VMEM),
        compiler_params=LIMIT,
    )(requests, arrived, attention_cotangent, next_block, weight)
    weight_other = swap(weight)

    before = lax.ppermute(last, "seq", [(at, at + 1) for at in range(owners - 1)])
    lower = jnp.concatenate([lower] + [shifted(lower, "tp", i) for i in range(1, tps)], 1)
    final_row = lax.broadcasted_iota(jnp.int32, before.shape, 0) == SPAN - 1
    upper = jnp.concatenate([jnp.where(final_row, upper[:SPAN], before), upper[SPAN:]])
    upper = jnp.concatenate([upper] + [shifted(upper, "grp", i) for i in range(1, grps)], 1)
    upper = [upper, shifted(upper, "tp", 1), shifted(upper, "tp", tps - 1)]
    lower = [lower, shifted(lower, "grp", 1), shifted(lower, "grp", grps - 1)]
    far = halves_round(upper[1], upper[2], "tp") + halves_round(lower[1], lower[2], "grp")
    all_stats = lax.all_to_all(
        jnp.broadcast_to(stats[None], (owners, *stats.shape)), "seq", split_axis=0, concat_axis=0, tiled=True
    ).reshape(owners * span_count, *stats.shape[1:])
    neighbour_gradient, finished = pl.pallas_call(
        functools.partial(pair_backward, 4),
        cost_estimate=cost(10),
        out_shape=(
            jax.ShapeDtypeStruct(neighbour_states.shape, jnp.bfloat16),
            jax.ShapeDtypeStruct((8, HDIM), jnp.float32),
        ),
        in_specs=[SMEM, ANY, ANY, VMEM, VMEM],
        out_specs=(VMEM, VMEM),
        scratch_shapes=[
            pltpu.VMEM(neighbour_states.shape, jnp.float32),
            pltpu.VMEM((2, owners * CAP, SPAN + 16, width), jnp.bfloat16),
            pltpu.SemaphoreType.DMA((2, owners * CAP)),
        ],
        compiler_params=WIDE,
    )(slots, all_queries, cotangents, neighbour_states, all_stats)
    total = pl.pallas_call(
        project_near,
        cost_estimate=cost(3),
        out_shape=jax.ShapeDtypeStruct((2, tok_rows, half), jnp.float32),
        in_specs=[VMEM] * 8 + [ANY],
        out_specs=VMEM,
        compiler_params=LIMIT,
    )(*upper, *lower, weight, weight_other, finished)
    layer_output = pl.pallas_call(
        project_far,
        cost_estimate=cost(2),
        out_shape=jax.ShapeDtypeStruct((tok_rows, out_columns), jnp.bfloat16),
        in_specs=[VMEM] * 7,
        out_specs=VMEM,
        compiler_params=LIMIT,
    )(*far, weight, weight_other, total)
    return (layer_output, neighbour_gradient)


def solution(mesh):
    placed = (
        P("seq", FEATS),
        P(None, "seq", None, FEATS),
        P("seq", None),
        P("seq", None),
        P(FEATS, None),
        P("seq", FEATS),
    )
    return jax.shard_map(
        local,
        mesh=mesh,
        in_specs=placed,
        out_specs=(P("seq", FEATS), P(None, "seq", None, FEATS)),
        check_vma=False,
    )
```

```python
import functools

import jax
import jax.numpy as jnp
from jax import lax
from jax.experimental import pallas as pl
from jax.experimental.pallas import tpu as pltpu
from jax.sharding import PartitionSpec as P

HDIM = 128
SPAN = 64
NTOK = 128
KNB = 2
CAP = 2
FEATS = ("grp", "tp")
LOG2E = 1.4426950408889634
NT = (((1,), (1,)), ((), ()))
NN = (((1,), (0,)), ((), ()))
TN = (((0,), (0,)), ((), ()))
VMEM = pl.BlockSpec(memory_space=pltpu.VMEM)
SMEM = pl.BlockSpec(memory_space=pltpu.SMEM)
ANY = pl.BlockSpec(memory_space=pl.ANY)
LIMIT = pltpu.CompilerParams(vmem_limit_bytes=48 * 1024 * 1024)


def cost(gigaflops):
    return pl.CostEstimate(flops=int(gigaflops * 1e9), bytes_accessed=8 * 1024 * 1024, transcendentals=0)


def dot(a, b, dims):
    return lax.dot_general(a, b, dims, preferred_element_type=jnp.float32)


def tied(value, *others):
    return pl.pallas_call(
        lambda *refs: None,
        out_shape=jax.ShapeDtypeStruct(value.shape, value.dtype),
        in_specs=[ANY] * (1 + len(others)),
        out_specs=ANY,
        input_output_aliases={0: 0},
    )(value, *others)


def decode_slot(code):
    return code & 127, (code >> 7) & 7, code >> 10


def span_tokens(window, span, spans):
    place = lax.broadcasted_iota(jnp.int32, (16, window.shape[1]), 0)
    first_token = (place == 15) & (span < spans - 1)
    tail = jnp.where(first_token, window[:16, :], window[SPAN:, :])
    return jnp.concatenate([window[16:SPAN, :], tail], 0)


def diagonal(first, second):
    zero = jnp.zeros_like(first)
    return jnp.concatenate(
        [jnp.concatenate([first, zero], 1), jnp.concatenate([zero, second], 1)], 0
    )


def span_forward(codes, queries, cotangents, store, upper, lower, stats, held, sems):
    blocks, width = queries.shape[0] // SPAN, queries.shape[1]
    windows = blocks + 1
    heads = range(0, width, HDIM)
    scale = HDIM ** (-0.5)
    copies = []
    for i in range(KNB * windows):
        row = codes[i] & 127
        source = store.at[lax.div(row, store.shape[2]), :, lax.rem(row, store.shape[2])]
        copies.append(pltpu.make_async_copy(source, held.at[i], sems.at[i]))
        copies[-1].start()

    lane = lax.broadcasted_iota(jnp.int32, (1, 2 * SPAN), 1)
    early = lane < SPAN
    place = lax.broadcasted_iota(jnp.int32, (16, width), 0)

    def window(ref, i):
        if i == 0 or i == blocks:
            at = min(i, blocks - 1) * SPAN
            return ref[at : at + SPAN, :]
        at = i * SPAN
        tail = jnp.where(place == 15, ref[at - 16 : at, :], ref[at + SPAN - 16 : at + SPAN, :])
        return jnp.concatenate([ref[at : at + SPAN - 16, :], tail], 0)

    attended, lines = {}, {}
    for first in range(0, windows, 2):
        second = min(first + 1, windows - 1)
        for i in range(KNB * first, KNB * (second + 1)):
            copies[i].wait()
        tokens = [window(queries, i) for i in (first, second)]
        others = [window(cotangents, i) for i in (first, second)]
        live = [jnp.where(early, codes[KNB * first + k] >> 7, codes[KNB * second + k] >> 7) > 0 for k in range(KNB)]
        for h, at in enumerate(heads):
            q = diagonal(*[each[:, at : at + HDIM] for each in tokens])
            g = diagonal(*[each[:, at : at + HDIM] for each in others])
            k, v = [
                jnp.concatenate(
                    [
                        jnp.concatenate([held[KNB * i + n, kind, :, at : at + HDIM] for n in range(KNB)], 0)
                        for i in (first, second)
                    ],
                    1,
                )
                for kind in range(2)
            ]
            scores = dot(k, q, NT)
            scores = [jnp.where(live[n], scores[n * NTOK : (n + 1) * NTOK], -1e30) for n in range(KNB)]
            top = jnp.max(jnp.maximum(scores[0], scores[1]), axis=0, keepdims=True)
            weights = [
                jnp.where(live[n], jnp.exp2((scores[n] - top) * (scale * LOG2E)), 0.0) for n in range(KNB)
            ]
            total = jnp.maximum(jnp.sum(weights[0] + weights[1], axis=0, keepdims=True), 1.0)
            weights = jnp.concatenate(weights, 0) * (1.0 / total)
            delta = jnp.sum(weights * dot(v, g, NT), axis=0, keepdims=True)
            mixed = dot(weights.astype(jnp.bfloat16), v, TN)
            attended[first, h], attended[second, h] = mixed[:SPAN, :HDIM], mixed[SPAN:, HDIM:]
            lines[first, h] = jnp.concatenate([top * scale + jnp.log(total), delta], 0)

    final_row = lax.broadcasted_iota(jnp.int32, (SPAN, width), 0) == SPAN - 1
    rolled = {key: pltpu.roll(jnp.concatenate([value] * 4, 0), SPAN, 1)[:2] for key, value in lines.items()}
    for i in range(blocks):
        mixed = [jnp.concatenate([attended[j, h] for h in range(len(heads))], 1) for j in (i, i + 1)]
        half, at = (upper, i) if i < blocks // 2 else (lower, i - blocks // 2)
        half[pl.ds(at * SPAN, SPAN), :] = jnp.where(final_row, mixed[1], mixed[0]).astype(half.dtype)
        rows = []
        for h in range(len(heads)):
            both = []
            for j in (i, i + 1):
                pair = (lines[j - j % 2, h], rolled[j - j % 2, h])
                both.append(jnp.where(early, pair[j % 2], pair[1 - j % 2]))
            rows.append(jnp.where(lane % SPAN == SPAN - 1, both[1], both[0]))
        stats[i] = jnp.concatenate([row[kind : kind + 1] for kind in range(2) for row in rows], 0)


def pair_backward(together, slots, rows, states, stats, *rest):
    out, total, windows, sems = rest[-4:]
    spans = stats.shape[0]
    reach = SPAN + 16
    copies = []
    for i in range(slots.shape[0]):
        span = decode_slot(slots[i])[0]
        start = jnp.minimum(span * SPAN + SPAN - 16, rows.shape[0] - reach)
        source = rows.at[pl.ds(pl.multiple_of(start, 16), reach)]
        copies.append(pltpu.make_async_copy(source, windows.at[i], sems.at[i]))
        copies[-1].start()
    total[...] = jnp.zeros_like(total)
    width = states.shape[3]
    heads = width // HDIM
    scale = HDIM ** (-0.5)
    lane = lax.broadcasted_iota(jnp.int32, (1, 2 * SPAN), 1)
    early = lane < SPAN
    first_token = lane % SPAN == SPAN - 1
    last_span = stats.shape[0] - 1

    def one_target(target):
        span_0, row_0, live_0 = decode_slot(slots[target * CAP])
        span_1, row_1, live_1 = decode_slot(slots[target * CAP + 1])
        tokens_0 = span_tokens(windows.at[target * CAP], span_0, spans)
        tokens_1 = span_tokens(windows.at[target * CAP + 1], span_1, spans)
        span = jnp.where(early, span_0, span_1)
        seen = (jnp.where(early, live_0, live_1) > 0) & (first_token | (span < last_span))
        lines = jnp.where(
            first_token,
            jnp.where(early, stats[span_0], stats[span_1]),
            jnp.where(
                early, stats[jnp.minimum(span_0 + 1, last_span)], stats[jnp.minimum(span_1 + 1, last_span)]
            ),
        )
        parts = []
        for h in range(heads):
            at = h * HDIM
            q = diagonal(tokens_0[:, at : at + HDIM], tokens_1[:, at : at + HDIM])
            g = diagonal(
                tokens_0[:, width + at : width + at + HDIM], tokens_1[:, width + at : width + at + HDIM]
            )
            k = jnp.concatenate([states[0, row_0, :, at : at + HDIM], states[0, row_1, :, at : at + HDIM]], 1)
            v = jnp.concatenate([states[1, row_0, :, at : at + HDIM], states[1, row_1, :, at : at + HDIM]], 1)
            scores = dot(k, q, NT) * scale
            weights = jnp.where(seen, jnp.exp(scores - lines[h : h + 1]), 0.0)
            grads = weights * (dot(v, g, NT) - lines[heads + h : heads + h + 1])
            key_part = dot(grads.astype(jnp.bfloat16), q, NN) * scale
            value_part = dot(weights.astype(jnp.bfloat16), g, NN)
            parts.append((key_part, value_part))
        return row_0, row_1, parts

    def some_targets(step, carry):
        for i in range(together * CAP):
            at = step * together * CAP + i
            pltpu.make_async_copy(rows.at[pl.ds(0, reach)], windows.at[at], sems.at[at]).wait()
        results = [one_target(step * together + i) for i in range(together)]
        for row_0, row_1, parts in results:
            for h, pair in enumerate(parts):
                for kind, part in enumerate(pair):
                    total[kind, row_0, :, h * HDIM : (h + 1) * HDIM] += part[:, :HDIM]
                    total[kind, row_1, :, h * HDIM : (h + 1) * HDIM] += part[:, HDIM:]
        return carry

    lax.fori_loop(0, slots.shape[0] // CAP // together, some_targets, 0)
    out[...] = total[...].astype(out.dtype)


def cut_weight(core, columns, block):
    count, _, half = block.shape
    for i in range(count):
        at = pl.multiple_of((2 * i + core[0]) * half, 128)
        block[i] = columns[:, pl.ds(at, half)]


def shifted(value, axis, steps):
    count = lax.axis_size(axis)
    return lax.ppermute(value, axis, [(source, (source + steps) % count) for source in range(count)])


def halves_round(first, second, axis):
    half = first.shape[1] // 2
    return [shifted(first[:, :half], axis, 1), shifted(second[:, half:], axis, lax.axis_size(axis) - 1)]


def source_of(steps_grp, steps_tp):
    grps, tps = lax.axis_size("grp"), lax.axis_size("tp")
    grp = lax.rem(lax.axis_index("grp") + (grps - steps_grp) % grps, grps)
    return grp * tps + lax.rem(lax.axis_index("tp") + (tps - steps_tp) % tps, tps)


def project_near(*refs):
    blocks, weights, out = refs[:6], refs[6:8], refs[-1]
    side = lax.axis_size("tp")
    rows, width = blocks[0].shape[0], weights[0].shape[1]
    for half in range(2):
        for kind, weight in enumerate(weights):
            total = None
            for block, step in zip(blocks[half * 3 : half * 3 + 3], (0, 1, side - 1)):
                for inner in range(side):
                    source = source_of(inner, step) if half == 0 else source_of(step, inner)
                    term = dot(block[:, inner * width : (inner + 1) * width], weight[source], NN)
                    total = term if total is None else total + term
            out[kind, pl.ds(half * rows, rows), :] = total


def project_far(*refs):
    blocks, weights, partial, out = refs[:4], refs[4:6], refs[6], refs[7]
    side = lax.axis_size("tp")
    rows, width = blocks[0].shape[0], weights[0].shape[1]
    columns = weights[0].shape[2]
    core = lax.rem(lax.axis_index("seq"), 2)
    for half in range(2):
        for kind, weight in enumerate(weights):
            total = partial[kind, pl.ds(half * rows, rows), :]
            for inner in range(side):
                block = blocks[half * 2 + inner // (side // 2)]
                at = inner % (side // 2) * width
                far = side // 2
                source = source_of(inner, far) if half == 0 else source_of(far, inner)
                total = total + dot(block[:, at : at + width], weight[source], NN)
            at = pl.multiple_of((core if kind == 0 else 1 - core) * columns, 128)
            out[pl.ds(half * rows, rows), pl.ds(at, columns)] = total.astype(out.dtype)


def local(queries, neighbour_states, retrieved, valid_blocks, output_weight, attention_cotangent):
    owners = lax.axis_size("seq")
    grps, tps = lax.axis_size("grp"), lax.axis_size("tp")
    me = lax.axis_index("seq")
    tok_rows, width = queries.shape
    span_count = tok_rows // SPAN
    request_count = span_count * KNB
    store_rows = neighbour_states.shape[1]
    out_columns = output_weight.shape[1] // (grps * tps)

    core = (me & 1).reshape(1)
    half = out_columns // 2
    sources = 4 if grps * tps % 4 == 0 else 1
    cut = pl.pallas_call(
        cut_weight,
        grid_spec=pltpu.PrefetchScalarGridSpec(
            num_scalar_prefetch=1,
            grid=(grps * tps // sources,),
            in_specs=[pl.BlockSpec((width, sources * out_columns), lambda i, core: (0, i))],
            out_specs=pl.BlockSpec((sources, width, half), lambda i, core: (i, 0, 0)),
        ),
        out_shape=jax.ShapeDtypeStruct((grps * tps, width, half), jnp.bfloat16),
    )(core, output_weight)
    weight = lax.all_to_all(cut, FEATS, split_axis=0, concat_axis=0, tiled=True)

    table = lax.all_gather(
        jnp.stack([retrieved.reshape(request_count), valid_blocks.reshape(request_count)]), "seq", axis=0
    )
    owner_of = table[:, 0] // store_rows
    same_owner = owner_of[:, :, None] == owner_of[:, None, :]
    order = jnp.arange(request_count, dtype=jnp.int32)
    earlier = order[None, :] < order[:, None]
    position = jnp.sum((same_owner & earlier[None]).astype(jnp.int32), axis=2)
    span_of = jnp.arange(owners, dtype=jnp.int32)[:, None] * span_count + order[None, :] // KNB
    code = span_of + 128 * (table[:, 0] % store_rows) + 1024 * (table[:, 1] > 0).astype(jnp.int32)
    hit = (owner_of == me)[:, None, :] & (
        position[:, None, :] == jnp.arange(CAP, dtype=jnp.int32)[None, :, None]
    )
    slots = jnp.sum(jnp.where(hit, code[:, None, :], 0), axis=2).reshape(owners * CAP)
    plain = (table[:, 0] + 128 * (table[:, 1] > 0).astype(jnp.int32)).reshape(owners * request_count)
    plain = jnp.concatenate([jnp.zeros((KNB,), jnp.int32), plain])
    codes = lax.dynamic_slice_in_dim(plain, me * request_count, request_count + KNB, 0)

    store = lax.all_gather(neighbour_states, "seq", axis=0)
    store = tied(store, slots, codes, weight)
    both = tied(jnp.concatenate([queries, attention_cotangent], axis=1), weight)
    gathered = lax.all_gather(both, "seq", axis=0, tiled=True)
    weight_other = lax.ppermute(weight, "seq", [(source, source ^ 1) for source in range(owners)])

    middle = tok_rows // 2
    upper, lower, stats = pl.pallas_call(
        span_forward,
        cost_estimate=cost(5),
        out_shape=(
            jax.ShapeDtypeStruct((middle, width), jnp.bfloat16),
            jax.ShapeDtypeStruct((middle, width), jnp.bfloat16),
            jax.ShapeDtypeStruct((span_count, 2 * width // HDIM, 2 * SPAN), jnp.float32),
        ),
        in_specs=[SMEM, VMEM, VMEM, ANY],
        out_specs=(VMEM, VMEM, VMEM),
        scratch_shapes=[
            pltpu.VMEM((request_count + KNB, 2, NTOK, width), jnp.bfloat16),
            pltpu.SemaphoreType.DMA((request_count + KNB,)),
        ],
        compiler_params=LIMIT,
    )(codes, queries, attention_cotangent, store)

    lower = jnp.concatenate([lower] + [shifted(lower, "tp", i) for i in range(1, tps)], 1)
    upper = jnp.concatenate([upper] + [shifted(upper, "grp", i) for i in range(1, grps)], 1)
    upper = [upper, shifted(upper, "tp", 1), shifted(upper, "tp", tps - 1)]
    lower = [lower, shifted(lower, "grp", 1), shifted(lower, "grp", grps - 1)]
    far = halves_round(upper[1], upper[2], "tp") + halves_round(lower[1], lower[2], "grp")
    total = pl.pallas_call(
        project_near,
        cost_estimate=cost(3),
        out_shape=jax.ShapeDtypeStruct((2, tok_rows, half), jnp.float32),
        in_specs=[VMEM] * 8,
        out_specs=VMEM,
        compiler_params=LIMIT,
    )(*upper, *lower, weight, weight_other)
    layer_output = pl.pallas_call(
        project_far,
        cost_estimate=cost(2),
        out_shape=jax.ShapeDtypeStruct((tok_rows, out_columns), jnp.bfloat16),
        in_specs=[VMEM] * 7,
        out_specs=VMEM,
        compiler_params=LIMIT,
    )(*far, weight, weight_other, total)

    all_stats = lax.all_to_all(
        jnp.broadcast_to(stats[None], (owners, *stats.shape)), "seq", split_axis=0, concat_axis=0, tiled=True
    ).reshape(owners * span_count, *stats.shape[1:])
    neighbour_gradient = pl.pallas_call(
        functools.partial(pair_backward, 4),
        cost_estimate=cost(10),
        out_shape=jax.ShapeDtypeStruct(neighbour_states.shape, jnp.bfloat16),
        in_specs=[SMEM, ANY, VMEM, VMEM, ANY],
        out_specs=VMEM,
        scratch_shapes=[
            pltpu.VMEM(neighbour_states.shape, jnp.float32),
            pltpu.VMEM((owners * CAP, SPAN + 16, 2 * width), jnp.bfloat16),
            pltpu.SemaphoreType.DMA((owners * CAP,)),
        ],
        compiler_params=LIMIT,
    )(slots, gathered, neighbour_states, all_stats, layer_output)
    return (layer_output, neighbour_gradient)


def solution(mesh):
    placed = (
        P("seq", FEATS),
        P(None, "seq", None, FEATS),
        P("seq", None),
        P("seq", None),
        P(FEATS, None),
        P("seq", FEATS),
    )
    return jax.shard_map(
        local,
        mesh=mesh,
        in_specs=placed,
        out_specs=(P("seq", FEATS), P(None, "seq", None, FEATS)),
        check_vma=False,
    )
```

```python
import functools

import jax
import jax.numpy as jnp
from jax import lax
from jax.experimental import pallas as pl
from jax.experimental.pallas import tpu as pltpu
from jax.sharding import PartitionSpec as P

HDIM = 128
SPAN = 64
NTOK = 128
KNB = 2
CAP = 2
FEATS = ("grp", "tp")
LOG2E = 1.4426950408889634
NT = (((1,), (1,)), ((), ()))
NN = (((1,), (0,)), ((), ()))
TN = (((0,), (0,)), ((), ()))
VMEM = pl.BlockSpec(memory_space=pltpu.VMEM)
SMEM = pl.BlockSpec(memory_space=pltpu.SMEM)
ANY = pl.BlockSpec(memory_space=pl.ANY)
LIMIT = pltpu.CompilerParams(vmem_limit_bytes=48 * 1024 * 1024)


def cost(gigaflops):
    return pl.CostEstimate(flops=int(gigaflops * 1e9), bytes_accessed=8 * 1024 * 1024, transcendentals=0)


def dot(a, b, dims):
    return lax.dot_general(a, b, dims, preferred_element_type=jnp.float32)


def tied(value, *others):
    return pl.pallas_call(
        lambda *refs: None,
        out_shape=jax.ShapeDtypeStruct(value.shape, value.dtype),
        in_specs=[ANY] * (1 + len(others)),
        out_specs=ANY,
        input_output_aliases={0: 0},
    )(value, *others)


def decode_slot(code):
    return code & 127, (code >> 7) & 7, code >> 10


def span_tokens(window, span, spans):
    place = lax.broadcasted_iota(jnp.int32, (16, window.shape[1]), 0)
    first_token = (place == 15) & (span < spans - 1)
    tail = jnp.where(first_token, window[:16, :], window[SPAN:, :])
    return jnp.concatenate([window[16:SPAN, :], tail], 0)


def diagonal(first, second):
    zero = jnp.zeros_like(first)
    return jnp.concatenate(
        [jnp.concatenate([first, zero], 1), jnp.concatenate([zero, second], 1)], 0
    )


def span_forward(codes, queries, cotangents, store, upper, lower, stats, held, sems):
    blocks, width = queries.shape[0] // SPAN, queries.shape[1]
    windows = blocks + 1
    heads = range(0, width, HDIM)
    scale = HDIM ** (-0.5)
    copies = []
    for i in range(KNB * windows):
        row = codes[i] & 127
        source = store.at[lax.div(row, store.shape[2]), :, lax.rem(row, store.shape[2])]
        copies.append(pltpu.make_async_copy(source, held.at[i], sems.at[i]))
        copies[-1].start()

    lane = lax.broadcasted_iota(jnp.int32, (1, 2 * SPAN), 1)
    early = lane < SPAN
    place = lax.broadcasted_iota(jnp.int32, (16, width), 0)

    def window(ref, i):
        if i == 0 or i == blocks:
            at = min(i, blocks - 1) * SPAN
            return ref[at : at + SPAN, :]
        at = i * SPAN
        tail = jnp.where(place == 15, ref[at - 16 : at, :], ref[at + SPAN - 16 : at + SPAN, :])
        return jnp.concatenate([ref[at : at + SPAN - 16, :], tail], 0)

    attended, lines = {}, {}
    for first in range(0, windows, 2):
        second = min(first + 1, windows - 1)
        for i in range(KNB * first, KNB * (second + 1)):
            copies[i].wait()
        tokens = [window(queries, i) for i in (first, second)]
        others = [window(cotangents, i) for i in (first, second)]
        live = [jnp.where(early, codes[KNB * first + k] >> 7, codes[KNB * second + k] >> 7) > 0 for k in range(KNB)]
        for h, at in enumerate(heads):
            q = diagonal(*[each[:, at : at + HDIM] for each in tokens])
            g = diagonal(*[each[:, at : at + HDIM] for each in others])
            k, v = [
                jnp.concatenate(
                    [
                        jnp.concatenate([held[KNB * i + n, kind, :, at : at + HDIM] for n in range(KNB)], 0)
                        for i in (first, second)
                    ],
                    1,
                )
                for kind in range(2)
            ]
            scores = dot(k, q, NT)
            scores = [jnp.where(live[n], scores[n * NTOK : (n + 1) * NTOK], -1e30) for n in range(KNB)]
            top = jnp.max(jnp.maximum(scores[0], scores[1]), axis=0, keepdims=True)
            weights = [
                jnp.where(live[n], jnp.exp2((scores[n] - top) * (scale * LOG2E)), 0.0) for n in range(KNB)
            ]
            total = jnp.maximum(jnp.sum(weights[0] + weights[1], axis=0, keepdims=True), 1.0)
            weights = jnp.concatenate(weights, 0) * (1.0 / total)
            delta = jnp.sum(weights * dot(v, g, NT), axis=0, keepdims=True)
            mixed = dot(weights.astype(jnp.bfloat16), v, TN)
            attended[first, h], attended[second, h] = mixed[:SPAN, :HDIM], mixed[SPAN:, HDIM:]
            lines[first, h] = jnp.concatenate([top * scale + jnp.log(total), delta], 0)

    final_row = lax.broadcasted_iota(jnp.int32, (SPAN, width), 0) == SPAN - 1
    rolled = {key: pltpu.roll(jnp.concatenate([value] * 4, 0), SPAN, 1)[:2] for key, value in lines.items()}
    for i in range(blocks):
        mixed = [jnp.concatenate([attended[j, h] for h in range(len(heads))], 1) for j in (i, i + 1)]
        half, at = (upper, i) if i < blocks // 2 else (lower, i - blocks // 2)
        half[pl.ds(at * SPAN, SPAN), :] = jnp.where(final_row, mixed[1], mixed[0]).astype(half.dtype)
        rows = []
        for h in range(len(heads)):
            both = []
            for j in (i, i + 1):
                pair = (lines[j - j % 2, h], rolled[j - j % 2, h])
                both.append(jnp.where(early, pair[j % 2], pair[1 - j % 2]))
            rows.append(jnp.where(lane % SPAN == SPAN - 1, both[1], both[0]))
        both = jnp.concatenate([row[kind : kind + 1] for kind in range(2) for row in rows], 0)
        if i % 2:
            stats[i // 2] = jnp.where(early, previous, both)
        previous = both


def pair_backward(together, slots, rows, states, stats, *rest):
    out, total, windows, sems = rest[-4:]
    spans = 2 * stats.shape[0]
    reach = SPAN + 16
    copies = []
    for i in range(slots.shape[0]):
        span = decode_slot(slots[i])[0]
        start = jnp.minimum(span * SPAN + SPAN - 16, rows.shape[0] - reach)
        source = rows.at[pl.ds(pl.multiple_of(start, 16), reach)]
        copies.append(pltpu.make_async_copy(source, windows.at[i], sems.at[i]))
        copies[-1].start()
    total[...] = jnp.zeros_like(total)
    width = states.shape[3]
    heads = width // HDIM
    scale = HDIM ** (-0.5)
    lane = lax.broadcasted_iota(jnp.int32, (1, 2 * SPAN), 1)
    early = lane < SPAN
    first_token = lane % SPAN == SPAN - 1
    last_span = spans - 1

    def block_lines(block):
        held = stats[block >> 1]
        turned = pltpu.roll(jnp.concatenate([held, held], 0), SPAN, 1)[: held.shape[0]]
        return jnp.where(early == ((block & 1) == 0), held, turned)

    def one_target(target):
        span_0, row_0, live_0 = decode_slot(slots[target * CAP])
        span_1, row_1, live_1 = decode_slot(slots[target * CAP + 1])
        tokens_0 = span_tokens(windows.at[target * CAP], span_0, spans)
        tokens_1 = span_tokens(windows.at[target * CAP + 1], span_1, spans)
        span = jnp.where(early, span_0, span_1)
        seen = (jnp.where(early, live_0, live_1) > 0) & (first_token | (span < last_span))
        lines = jnp.where(
            first_token,
            jnp.where(early, block_lines(span_0), block_lines(span_1)),
            jnp.where(
                early,
                block_lines(jnp.minimum(span_0 + 1, last_span)),
                block_lines(jnp.minimum(span_1 + 1, last_span)),
            ),
        )
        parts = []
        for h in range(heads):
            at = h * HDIM
            q = diagonal(tokens_0[:, at : at + HDIM], tokens_1[:, at : at + HDIM])
            g = diagonal(
                tokens_0[:, width + at : width + at + HDIM], tokens_1[:, width + at : width + at + HDIM]
            )
            k = jnp.concatenate([states[0, row_0, :, at : at + HDIM], states[0, row_1, :, at : at + HDIM]], 1)
            v = jnp.concatenate([states[1, row_0, :, at : at + HDIM], states[1, row_1, :, at : at + HDIM]], 1)
            both = dot(jnp.concatenate([k, v], 0), jnp.concatenate([q, g], 0), NT)
            scores = both[:NTOK, : 2 * SPAN] * scale
            weights = jnp.where(seen, jnp.exp(scores - lines[h : h + 1]), 0.0)
            grads = weights * (both[NTOK:, 2 * SPAN :] - lines[heads + h : heads + h + 1])
            key_part = dot(grads.astype(jnp.bfloat16), q, NN) * scale
            value_part = dot(weights.astype(jnp.bfloat16), g, NN)
            parts.append((key_part, value_part))
        return row_0, row_1, parts

    def some_targets(step, carry):
        for i in range(together * CAP):
            at = step * together * CAP + i
            pltpu.make_async_copy(rows.at[pl.ds(0, reach)], windows.at[at], sems.at[at]).wait()
        results = [one_target(step * together + i) for i in range(together)]
        for row_0, row_1, parts in results:
            for h, pair in enumerate(parts):
                for kind, part in enumerate(pair):
                    total[kind, row_0, :, h * HDIM : (h + 1) * HDIM] += part[:, :HDIM]
                    total[kind, row_1, :, h * HDIM : (h + 1) * HDIM] += part[:, HDIM:]
        return carry

    lax.fori_loop(0, slots.shape[0] // CAP // together, some_targets, 0)
    out[...] = total[...].astype(out.dtype)


def cut_weight(core, columns, block):
    count, _, half = block.shape
    for i in range(count):
        at = pl.multiple_of((2 * i + core[0]) * half, 128)
        block[i] = columns[:, pl.ds(at, half)]


def shifted(value, axis, steps):
    count = lax.axis_size(axis)
    return lax.ppermute(value, axis, [(source, (source + steps) % count) for source in range(count)])


def halves_round(first, second, axis):
    half = first.shape[1] // 2
    return [shifted(first[:, :half], axis, 1), shifted(second[:, half:], axis, lax.axis_size(axis) - 1)]


def source_of(steps_grp, steps_tp):
    grps, tps = lax.axis_size("grp"), lax.axis_size("tp")
    grp = lax.rem(lax.axis_index("grp") + (grps - steps_grp) % grps, grps)
    return grp * tps + lax.rem(lax.axis_index("tp") + (tps - steps_tp) % tps, tps)


def project_near(*refs):
    blocks, weights, out = refs[:6], refs[6:8], refs[-1]
    side = lax.axis_size("tp")
    rows, width = blocks[0].shape[0], weights[0].shape[1]
    for half in range(2):
        for kind, weight in enumerate(weights):
            total = None
            for block, step in zip(blocks[half * 3 : half * 3 + 3], (0, 1, side - 1)):
                for inner in range(side):
                    source = source_of(inner, step) if half == 0 else source_of(step, inner)
                    term = dot(block[:, inner * width : (inner + 1) * width], weight[source], NN)
                    total = term if total is None else total + term
            out[kind, pl.ds(half * rows, rows), :] = total


def project_far(*refs):
    blocks, weights, partial, out, finished = refs[:4], refs[4:6], refs[6], refs[7], refs[8]
    finished[...] = jnp.zeros_like(finished)
    side = lax.axis_size("tp")
    rows, width = blocks[0].shape[0], weights[0].shape[1]
    columns = weights[0].shape[2]
    core = lax.rem(lax.axis_index("seq"), 2)
    for half in range(2):
        for kind, weight in enumerate(weights):
            total = partial[kind, pl.ds(half * rows, rows), :]
            for inner in range(side):
                block = blocks[half * 2 + inner // (side // 2)]
                at = inner % (side // 2) * width
                far = side // 2
                source = source_of(inner, far) if half == 0 else source_of(far, inner)
                total = total + dot(block[:, at : at + width], weight[source], NN)
            at = pl.multiple_of((core if kind == 0 else 1 - core) * columns, 128)
            out[pl.ds(half * rows, rows), pl.ds(at, columns)] = total.astype(out.dtype)


def local(queries, neighbour_states, retrieved, valid_blocks, output_weight, attention_cotangent):
    owners = lax.axis_size("seq")
    grps, tps = lax.axis_size("grp"), lax.axis_size("tp")
    me = lax.axis_index("seq")
    tok_rows, width = queries.shape
    span_count = tok_rows // SPAN
    request_count = span_count * KNB
    store_rows = neighbour_states.shape[1]
    out_columns = output_weight.shape[1] // (grps * tps)

    core = (me & 1).reshape(1)
    half = out_columns // 2
    sources = 4 if grps * tps % 4 == 0 else 1
    cut = pl.pallas_call(
        cut_weight,
        grid_spec=pltpu.PrefetchScalarGridSpec(
            num_scalar_prefetch=1,
            grid=(grps * tps // sources,),
            in_specs=[pl.BlockSpec((width, sources * out_columns), lambda i, core: (0, i))],
            out_specs=pl.BlockSpec((sources, width, half), lambda i, core: (i, 0, 0)),
        ),
        out_shape=jax.ShapeDtypeStruct((grps * tps, width, half), jnp.bfloat16),
    )(core, output_weight)
    weight = lax.all_to_all(cut, FEATS, split_axis=0, concat_axis=0, tiled=True)

    table = lax.all_gather(
        jnp.stack([retrieved.reshape(request_count), valid_blocks.reshape(request_count)]), "seq", axis=0
    )
    owner_of = table[:, 0] // store_rows
    same_owner = owner_of[:, :, None] == owner_of[:, None, :]
    order = jnp.arange(request_count, dtype=jnp.int32)
    earlier = order[None, :] < order[:, None]
    position = jnp.sum((same_owner & earlier[None]).astype(jnp.int32), axis=2)
    span_of = jnp.arange(owners, dtype=jnp.int32)[:, None] * span_count + order[None, :] // KNB
    code = span_of + 128 * (table[:, 0] % store_rows) + 1024 * (table[:, 1] > 0).astype(jnp.int32)
    hit = (owner_of == me)[:, None, :] & (
        position[:, None, :] == jnp.arange(CAP, dtype=jnp.int32)[None, :, None]
    )
    slots = jnp.sum(jnp.where(hit, code[:, None, :], 0), axis=2).reshape(owners * CAP)
    plain = (table[:, 0] + 128 * (table[:, 1] > 0).astype(jnp.int32)).reshape(owners * request_count)
    plain = jnp.concatenate([jnp.zeros((KNB,), jnp.int32), plain])
    codes = lax.dynamic_slice_in_dim(plain, me * request_count, request_count + KNB, 0)

    store = lax.all_gather(neighbour_states, "seq", axis=0)
    store = tied(store, slots, codes, weight)
    both = tied(jnp.concatenate([queries, attention_cotangent], axis=1), weight)
    gathered = lax.all_gather(both, "seq", axis=0, tiled=True)
    weight_other = lax.ppermute(weight, "seq", [(source, source ^ 1) for source in range(owners)])

    middle = tok_rows // 2
    upper, lower, stats = pl.pallas_call(
        span_forward,
        cost_estimate=cost(5),
        out_shape=(
            jax.ShapeDtypeStruct((middle, width), jnp.bfloat16),
            jax.ShapeDtypeStruct((middle, width), jnp.bfloat16),
            jax.ShapeDtypeStruct((span_count // 2, 2 * width // HDIM, 2 * SPAN), jnp.float32),
        ),
        in_specs=[SMEM, VMEM, VMEM, ANY],
        out_specs=(VMEM, VMEM, VMEM),
        scratch_shapes=[
            pltpu.VMEM((request_count + KNB, 2, NTOK, width), jnp.bfloat16),
            pltpu.SemaphoreType.DMA((request_count + KNB,)),
        ],
        compiler_params=LIMIT,
    )(codes, queries, attention_cotangent, store)

    lower = jnp.concatenate([lower] + [shifted(lower, "tp", i) for i in range(1, tps)], 1)
    upper = jnp.concatenate([upper] + [shifted(upper, "grp", i) for i in range(1, grps)], 1)
    upper = [upper, shifted(upper, "tp", 1), shifted(upper, "tp", tps - 1)]
    lower = [lower, shifted(lower, "grp", 1), shifted(lower, "grp", grps - 1)]
    far = halves_round(upper[1], upper[2], "tp") + halves_round(lower[1], lower[2], "grp")
    total = pl.pallas_call(
        project_near,
        cost_estimate=cost(3),
        out_shape=jax.ShapeDtypeStruct((2, tok_rows, half), jnp.float32),
        in_specs=[VMEM] * 8,
        out_specs=VMEM,
        compiler_params=LIMIT,
    )(*upper, *lower, weight, weight_other)
    layer_output, finished = pl.pallas_call(
        project_far,
        cost_estimate=cost(2),
        out_shape=(
            jax.ShapeDtypeStruct((tok_rows, out_columns), jnp.bfloat16),
            jax.ShapeDtypeStruct((8, HDIM), jnp.float32),
        ),
        in_specs=[VMEM] * 7,
        out_specs=(VMEM, VMEM),
        compiler_params=LIMIT,
    )(*far, weight, weight_other, total)

    all_stats = lax.all_to_all(
        jnp.broadcast_to(stats[None], (owners, *stats.shape)), "seq", split_axis=0, concat_axis=0, tiled=True
    ).reshape(owners * span_count // 2, *stats.shape[1:])
    neighbour_gradient = pl.pallas_call(
        functools.partial(pair_backward, 4),
        cost_estimate=cost(10),
        out_shape=jax.ShapeDtypeStruct(neighbour_states.shape, jnp.bfloat16),
        in_specs=[SMEM, ANY, VMEM, VMEM, VMEM],
        out_specs=VMEM,
        scratch_shapes=[
            pltpu.VMEM(neighbour_states.shape, jnp.float32),
            pltpu.VMEM((owners * CAP, SPAN + 16, 2 * width), jnp.bfloat16),
            pltpu.SemaphoreType.DMA((owners * CAP,)),
        ],
        compiler_params=LIMIT,
    )(slots, gathered, neighbour_states, all_stats, finished)
    return (layer_output, neighbour_gradient)


def solution(mesh):
    placed = (
        P("seq", FEATS),
        P(None, "seq", None, FEATS),
        P("seq", None),
        P("seq", None),
        P(FEATS, None),
        P("seq", FEATS),
    )
    return jax.shard_map(
        local,
        mesh=mesh,
        in_specs=placed,
        out_specs=(P("seq", FEATS), P(None, "seq", None, FEATS)),
        check_vma=False,
    )
```

```python
import functools

import jax
import jax.numpy as jnp
from jax import lax
from jax.experimental import pallas as pl
from jax.experimental.pallas import tpu as pltpu
from jax.sharding import PartitionSpec as P

HDIM = 128
SPAN = 64
NTOK = 128
KNB = 2
CAP = 2
FEATS = ("grp", "tp")
LOG2E = 1.4426950408889634
NT = (((1,), (1,)), ((), ()))
NN = (((1,), (0,)), ((), ()))
TN = (((0,), (0,)), ((), ()))
VMEM = pl.BlockSpec(memory_space=pltpu.VMEM)
SMEM = pl.BlockSpec(memory_space=pltpu.SMEM)
ANY = pl.BlockSpec(memory_space=pl.ANY)
LIMIT = pltpu.CompilerParams(vmem_limit_bytes=48 * 1024 * 1024)


def cost(gigaflops):
    return pl.CostEstimate(flops=int(gigaflops * 1e9), bytes_accessed=8 * 1024 * 1024, transcendentals=0)


def dot(a, b, dims):
    return lax.dot_general(a, b, dims, preferred_element_type=jnp.float32)


def tied(value, *others):
    return pl.pallas_call(
        lambda *refs: None,
        out_shape=jax.ShapeDtypeStruct(value.shape, value.dtype),
        in_specs=[ANY] * (1 + len(others)),
        out_specs=ANY,
        input_output_aliases={0: 0},
    )(value, *others)


def decode_slot(code):
    return code & 127, (code >> 7) & 7, code >> 10


def span_tokens(window, span, spans):
    place = lax.broadcasted_iota(jnp.int32, (16, window.shape[1]), 0)
    first_token = (place == 15) & (span < spans - 1)
    tail = jnp.where(first_token, window[:16, :], window[SPAN:, :])
    return jnp.concatenate([window[16:SPAN, :], tail], 0)


def diagonal(first, second):
    zero = jnp.zeros_like(first)
    return jnp.concatenate(
        [jnp.concatenate([first, zero], 1), jnp.concatenate([zero, second], 1)], 0
    )


def span_forward(distances, codes, queries, cotangents, store, *rest):
    pieces, (upper, lower, stats, held, extra, sems, extra_sems) = rest[:-7], rest[-7:]
    per_core = len(pieces) // 2
    me = lax.axis_index("seq")
    chips = lax.axis_size("seq") // 2
    piece_copies = []
    for i, piece in enumerate(pieces):
        distance, start = distances[i % per_core]
        chip = lax.rem(lax.div(me, 2) + (chips - distance) % chips, chips)
        core = lax.rem(lax.rem(me, 2) + i // per_core, 2)
        target = extra.at[chip * 2 + core, pl.ds(start, piece.shape[0])]
        piece_copies.append(pltpu.make_async_copy(piece, target, extra_sems.at[i]))
        piece_copies[-1].start()
    store_rows = (store.shape[1] + extra.shape[1] // NTOK) // 2
    value_rows = store.shape[1] - store_rows
    blocks, width = queries.shape[0] // SPAN, queries.shape[1]
    windows = blocks + 1
    heads = range(0, width, HDIM)
    scale = HDIM ** (-0.5)
    copies = []
    owners, rows = [], []
    for i in range(KNB * windows):
        row = codes[i] & 127
        owners.append(lax.div(row, store_rows))
        rows.append(lax.rem(row, store_rows))
        copies.append(pltpu.make_async_copy(store.at[owners[i], rows[i]], held.at[i, 0], sems.at[i, 0]))
        copies[-1].start()
    for copy in piece_copies:
        copy.wait()
    for i in range(KNB * windows):
        early_row = jnp.minimum(rows[i], value_rows - 1)
        late_row = pl.multiple_of(jnp.maximum(rows[i] - value_rows, 0) * NTOK, NTOK)
        stored = pltpu.make_async_copy(
            store.at[owners[i], store_rows + early_row], held.at[i, 1], sems.at[i, 1]
        )
        moved = pltpu.make_async_copy(
            extra.at[owners[i], pl.ds(late_row, NTOK)], held.at[i, 1], sems.at[i, 1]
        )
        pl.when(rows[i] < value_rows)(stored.start)
        pl.when(rows[i] >= value_rows)(moved.start)
        copies.append(stored)

    lane = lax.broadcasted_iota(jnp.int32, (1, 2 * SPAN), 1)
    early = lane < SPAN
    place = lax.broadcasted_iota(jnp.int32, (16, width), 0)

    def window(ref, i):
        if i == 0 or i == blocks:
            at = min(i, blocks - 1) * SPAN
            return ref[at : at + SPAN, :]
        at = i * SPAN
        tail = jnp.where(place == 15, ref[at - 16 : at, :], ref[at + SPAN - 16 : at + SPAN, :])
        return jnp.concatenate([ref[at : at + SPAN - 16, :], tail], 0)

    attended, lines = {}, {}
    for first in range(0, windows, 2):
        second = min(first + 1, windows - 1)
        for i in range(KNB * first, KNB * (second + 1)):
            copies[i].wait()
            copies[KNB * windows + i].wait()
        tokens = [window(queries, i) for i in (first, second)]
        others = [window(cotangents, i) for i in (first, second)]
        live = [jnp.where(early, codes[KNB * first + k] >> 7, codes[KNB * second + k] >> 7) > 0 for k in range(KNB)]
        for h, at in enumerate(heads):
            q = diagonal(*[each[:, at : at + HDIM] for each in tokens])
            g = diagonal(*[each[:, at : at + HDIM] for each in others])
            k, v = [
                jnp.concatenate(
                    [
                        jnp.concatenate([held[KNB * i + n, kind, :, at : at + HDIM] for n in range(KNB)], 0)
                        for i in (first, second)
                    ],
                    1,
                )
                for kind in range(2)
            ]
            scores = dot(k, q, NT)
            scores = [jnp.where(live[n], scores[n * NTOK : (n + 1) * NTOK], -1e30) for n in range(KNB)]
            top = jnp.max(jnp.maximum(scores[0], scores[1]), axis=0, keepdims=True)
            weights = [
                jnp.where(live[n], jnp.exp2((scores[n] - top) * (scale * LOG2E)), 0.0) for n in range(KNB)
            ]
            total = jnp.maximum(jnp.sum(weights[0] + weights[1], axis=0, keepdims=True), 1.0)
            weights = jnp.concatenate(weights, 0) * (1.0 / total)
            delta = jnp.sum(weights * dot(v, g, NT), axis=0, keepdims=True)
            mixed = dot(weights.astype(jnp.bfloat16), v, TN)
            attended[first, h], attended[second, h] = mixed[:SPAN, :HDIM], mixed[SPAN:, HDIM:]
            lines[first, h] = jnp.concatenate([top * scale + jnp.log(total), delta], 0)

    final_row = lax.broadcasted_iota(jnp.int32, (SPAN, width), 0) == SPAN - 1
    rolled = {key: pltpu.roll(jnp.concatenate([value] * 4, 0), SPAN, 1)[:2] for key, value in lines.items()}
    for i in range(blocks):
        mixed = [jnp.concatenate([attended[j, h] for h in range(len(heads))], 1) for j in (i, i + 1)]
        half, at = (upper, i) if i < blocks // 2 else (lower, i - blocks // 2)
        half[pl.ds(at * SPAN, SPAN), :] = jnp.where(final_row, mixed[1], mixed[0]).astype(half.dtype)
        rows = []
        for h in range(len(heads)):
            both = []
            for j in (i, i + 1):
                pair = (lines[j - j % 2, h], rolled[j - j % 2, h])
                both.append(jnp.where(early, pair[j % 2], pair[1 - j % 2]))
            rows.append(jnp.where(lane % SPAN == SPAN - 1, both[1], both[0]))
        both = jnp.concatenate([row[kind : kind + 1] for kind in range(2) for row in rows], 0)
        if i % 2:
            stats[i // 2] = jnp.where(early, previous, both)
        previous = both


def pair_backward(together, slots, rows, states, stats, *rest):
    out, total, windows, sems = rest[-4:]
    spans = 2 * stats.shape[0]
    reach = SPAN + 16
    copies = []
    for i in range(slots.shape[0]):
        span = decode_slot(slots[i])[0]
        start = jnp.minimum(span * SPAN + SPAN - 16, rows.shape[0] - reach)
        source = rows.at[pl.ds(pl.multiple_of(start, 16), reach)]
        copies.append(pltpu.make_async_copy(source, windows.at[i], sems.at[i]))
        copies[-1].start()
    total[...] = jnp.zeros_like(total)
    width = states.shape[3]
    heads = width // HDIM
    scale = HDIM ** (-0.5)
    lane = lax.broadcasted_iota(jnp.int32, (1, 2 * SPAN), 1)
    early = lane < SPAN
    first_token = lane % SPAN == SPAN - 1
    last_span = spans - 1

    def block_lines(block):
        held = stats[block >> 1]
        turned = pltpu.roll(jnp.concatenate([held, held], 0), SPAN, 1)[: held.shape[0]]
        return jnp.where(early == ((block & 1) == 0), held, turned)

    def one_target(target):
        span_0, row_0, live_0 = decode_slot(slots[target * CAP])
        span_1, row_1, live_1 = decode_slot(slots[target * CAP + 1])
        tokens_0 = span_tokens(windows.at[target * CAP], span_0, spans)
        tokens_1 = span_tokens(windows.at[target * CAP + 1], span_1, spans)
        span = jnp.where(early, span_0, span_1)
        seen = (jnp.where(early, live_0, live_1) > 0) & (first_token | (span < last_span))
        lines = jnp.where(
            first_token,
            jnp.where(early, block_lines(span_0), block_lines(span_1)),
            jnp.where(
                early,
                block_lines(jnp.minimum(span_0 + 1, last_span)),
                block_lines(jnp.minimum(span_1 + 1, last_span)),
            ),
        )
        parts = []
        for h in range(heads):
            at = h * HDIM
            q = diagonal(tokens_0[:, at : at + HDIM], tokens_1[:, at : at + HDIM])
            g = diagonal(
                tokens_0[:, width + at : width + at + HDIM], tokens_1[:, width + at : width + at + HDIM]
            )
            k = jnp.concatenate([states[0, row_0, :, at : at + HDIM], states[0, row_1, :, at : at + HDIM]], 1)
            v = jnp.concatenate([states[1, row_0, :, at : at + HDIM], states[1, row_1, :, at : at + HDIM]], 1)
            both = dot(jnp.concatenate([k, v], 0), jnp.concatenate([q, g], 0), NT)
            scores = both[:NTOK, : 2 * SPAN] * scale
            weights = jnp.where(seen, jnp.exp(scores - lines[h : h + 1]), 0.0)
            grads = weights * (both[NTOK:, 2 * SPAN :] - lines[heads + h : heads + h + 1])
            key_part = dot(grads.astype(jnp.bfloat16), q, NN) * scale
            value_part = dot(weights.astype(jnp.bfloat16), g, NN)
            parts.append((key_part, value_part))
        return row_0, row_1, parts

    def some_targets(step, carry):
        for i in range(together * CAP):
            at = step * together * CAP + i
            pltpu.make_async_copy(rows.at[pl.ds(0, reach)], windows.at[at], sems.at[at]).wait()
        results = [one_target(step * together + i) for i in range(together)]
        for row_0, row_1, parts in results:
            for h, pair in enumerate(parts):
                for kind, part in enumerate(pair):
                    total[kind, row_0, :, h * HDIM : (h + 1) * HDIM] += part[:, :HDIM]
                    total[kind, row_1, :, h * HDIM : (h + 1) * HDIM] += part[:, HDIM:]
        return carry

    lax.fori_loop(0, slots.shape[0] // CAP // together, some_targets, 0)
    out[...] = total[...].astype(out.dtype)


def cut_weight(core, columns, block):
    count, _, half = block.shape
    for i in range(count):
        at = pl.multiple_of((2 * i + core[0]) * half, 128)
        block[i] = columns[:, pl.ds(at, half)]


def shifted(value, axis, steps):
    count = lax.axis_size(axis)
    return lax.ppermute(value, axis, [(source, (source + steps) % count) for source in range(count)])


def halves_round(first, second, axis):
    half = first.shape[1] // 2
    return [shifted(first[:, :half], axis, 1), shifted(second[:, half:], axis, lax.axis_size(axis) - 1)]


def source_of(steps_grp, steps_tp):
    grps, tps = lax.axis_size("grp"), lax.axis_size("tp")
    grp = lax.rem(lax.axis_index("grp") + (grps - steps_grp) % grps, grps)
    return grp * tps + lax.rem(lax.axis_index("tp") + (tps - steps_tp) % tps, tps)


def project_near(*refs):
    blocks, weights, out = refs[:6], refs[6:8], refs[-1]
    side = lax.axis_size("tp")
    rows, width = blocks[0].shape[0], weights[0].shape[1]
    for half in range(2):
        for kind, weight in enumerate(weights):
            total = None
            for block, step in zip(blocks[half * 3 : half * 3 + 3], (0, 1, side - 1)):
                for inner in range(side):
                    source = source_of(inner, step) if half == 0 else source_of(step, inner)
                    term = dot(block[:, inner * width : (inner + 1) * width], weight[source], NN)
                    total = term if total is None else total + term
            out[kind, pl.ds(half * rows, rows), :] = total


def project_far(*refs):
    blocks, weights, partial, out, finished = refs[:4], refs[4:6], refs[6], refs[7], refs[8]
    finished[...] = jnp.zeros_like(finished)
    side = lax.axis_size("tp")
    rows, width = blocks[0].shape[0], weights[0].shape[1]
    columns = weights[0].shape[2]
    core = lax.rem(lax.axis_index("seq"), 2)
    for half in range(2):
        for kind, weight in enumerate(weights):
            total = partial[kind, pl.ds(half * rows, rows), :]
            for inner in range(side):
                block = blocks[half * 2 + inner // (side // 2)]
                at = inner % (side // 2) * width
                far = side // 2
                source = source_of(inner, far) if half == 0 else source_of(far, inner)
                total = total + dot(block[:, at : at + width], weight[source], NN)
            at = pl.multiple_of((core if kind == 0 else 1 - core) * columns, 128)
            out[pl.ds(half * rows, rows), pl.ds(at, columns)] = total.astype(out.dtype)


def local(queries, neighbour_states, retrieved, valid_blocks, output_weight, attention_cotangent):
    owners = lax.axis_size("seq")
    grps, tps = lax.axis_size("grp"), lax.axis_size("tp")
    me = lax.axis_index("seq")
    tok_rows, width = queries.shape
    span_count = tok_rows // SPAN
    request_count = span_count * KNB
    store_rows = neighbour_states.shape[1]
    out_columns = output_weight.shape[1] // (grps * tps)

    core = (me & 1).reshape(1)
    half = out_columns // 2
    sources = 4 if grps * tps % 4 == 0 else 1
    cut = pl.pallas_call(
        cut_weight,
        grid_spec=pltpu.PrefetchScalarGridSpec(
            num_scalar_prefetch=1,
            grid=(grps * tps // sources,),
            in_specs=[pl.BlockSpec((width, sources * out_columns), lambda i, core: (0, i))],
            out_specs=pl.BlockSpec((sources, width, half), lambda i, core: (i, 0, 0)),
        ),
        out_shape=jax.ShapeDtypeStruct((grps * tps, width, half), jnp.bfloat16),
    )(core, output_weight)
    weight = lax.all_to_all(cut, FEATS, split_axis=0, concat_axis=0, tiled=True)

    def steps(value, chips):
        return lax.ppermute(value, "seq", [(at, (at + 2 * chips) % owners) for at in range(owners)])

    def swap(value):
        return lax.ppermute(value, "seq", [(at, at ^ 1) for at in range(owners)])

    stacked = neighbour_states.reshape(2 * store_rows, NTOK, width)
    late_rows = store_rows // 2
    store = lax.all_gather(stacked[: 2 * store_rows - late_rows], "seq", axis=0)
    late = tied(stacked[2 * store_rows - late_rows :].reshape(late_rows * NTOK, width), cut)
    cut_at = late_rows * NTOK // 2
    up_1, down_1, up_2, down_2 = [steps(late, i) for i in (1, -1, 2, -2)]
    further = [steps(up_2, 1), steps(down_2, -1), steps(up_2[:cut_at], 2), steps(down_2[cut_at:], -2)]
    distances = [(0, 0), (1, 0), (-1, 0), (2, 0), (-2, 0), (3, 0), (-3, 0), (4, 0), (4, cut_at)]
    late = [late, up_1, down_1, up_2, down_2, *further]
    late = late + [swap(piece) for piece in late]
    table = jnp.stack([retrieved.reshape(request_count), valid_blocks.reshape(request_count)])
    table = lax.all_gather(tied(table, up_2, down_2), "seq", axis=0)
    owner_of = table[:, 0] // store_rows
    same_owner = owner_of[:, :, None] == owner_of[:, None, :]
    order = jnp.arange(request_count, dtype=jnp.int32)
    earlier = order[None, :] < order[:, None]
    position = jnp.sum((same_owner & earlier[None]).astype(jnp.int32), axis=2)
    span_of = jnp.arange(owners, dtype=jnp.int32)[:, None] * span_count + order[None, :] // KNB
    code = span_of + 128 * (table[:, 0] % store_rows) + 1024 * (table[:, 1] > 0).astype(jnp.int32)
    hit = (owner_of == me)[:, None, :] & (
        position[:, None, :] == jnp.arange(CAP, dtype=jnp.int32)[None, :, None]
    )
    slots = jnp.sum(jnp.where(hit, code[:, None, :], 0), axis=2).reshape(owners * CAP)
    codes = (retrieved + 128 * (valid_blocks > 0).astype(jnp.int32)).reshape(request_count)
    before = lax.ppermute(codes[-KNB:], "seq", [(at, at + 1) for at in range(owners - 1)])
    codes = jnp.concatenate([before, codes])

    store = tied(store, codes, slots)
    both = tied(jnp.concatenate([queries, attention_cotangent], axis=1), slots)
    gathered = lax.all_gather(both, "seq", axis=0, tiled=True)

    middle = tok_rows // 2
    upper, lower, stats = pl.pallas_call(
        functools.partial(span_forward, distances),
        cost_estimate=cost(5),
        out_shape=(
            jax.ShapeDtypeStruct((middle, width), jnp.bfloat16),
            jax.ShapeDtypeStruct((middle, width), jnp.bfloat16),
            jax.ShapeDtypeStruct((span_count // 2, 2 * width // HDIM, 2 * SPAN), jnp.float32),
        ),
        in_specs=[SMEM, VMEM, VMEM, ANY] + [ANY] * len(late),
        out_specs=(VMEM, VMEM, VMEM),
        scratch_shapes=[
            pltpu.VMEM((request_count + KNB, 2, NTOK, width), jnp.bfloat16),
            pltpu.VMEM((owners, late_rows * NTOK, width), jnp.bfloat16),
            pltpu.SemaphoreType.DMA((request_count + KNB, 2)),
            pltpu.SemaphoreType.DMA((len(late),)),
        ],
        compiler_params=LIMIT,
    )(codes, queries, attention_cotangent, store, *late)

    weight = tied(weight, stats)
    weight_other = swap(weight)
    lower = jnp.concatenate([lower] + [shifted(lower, "tp", i) for i in range(1, tps)], 1)
    upper = jnp.concatenate([upper] + [shifted(upper, "grp", i) for i in range(1, grps)], 1)
    upper = [upper, shifted(upper, "tp", 1), shifted(upper, "tp", tps - 1)]
    lower = [lower, shifted(lower, "grp", 1), shifted(lower, "grp", grps - 1)]
    far = halves_round(upper[1], upper[2], "tp") + halves_round(lower[1], lower[2], "grp")
    total = pl.pallas_call(
        project_near,
        cost_estimate=cost(3),
        out_shape=jax.ShapeDtypeStruct((2, tok_rows, half), jnp.float32),
        in_specs=[VMEM] * 8,
        out_specs=VMEM,
        compiler_params=LIMIT,
    )(*upper, *lower, weight, weight_other)
    layer_output, finished = pl.pallas_call(
        project_far,
        cost_estimate=cost(2),
        out_shape=(
            jax.ShapeDtypeStruct((tok_rows, out_columns), jnp.bfloat16),
            jax.ShapeDtypeStruct((8, HDIM), jnp.float32),
        ),
        in_specs=[VMEM] * 7,
        out_specs=(VMEM, VMEM),
        compiler_params=LIMIT,
    )(*far, weight, weight_other, total)

    all_stats = lax.all_to_all(
        jnp.broadcast_to(stats[None], (owners, *stats.shape)), "seq", split_axis=0, concat_axis=0, tiled=True
    ).reshape(owners * span_count // 2, *stats.shape[1:])
    neighbour_gradient = pl.pallas_call(
        functools.partial(pair_backward, 8),
        cost_estimate=cost(10),
        out_shape=jax.ShapeDtypeStruct(neighbour_states.shape, jnp.bfloat16),
        in_specs=[SMEM, ANY, VMEM, VMEM, VMEM],
        out_specs=VMEM,
        scratch_shapes=[
            pltpu.VMEM(neighbour_states.shape, jnp.float32),
            pltpu.VMEM((owners * CAP, SPAN + 16, 2 * width), jnp.bfloat16),
            pltpu.SemaphoreType.DMA((owners * CAP,)),
        ],
        compiler_params=LIMIT,
    )(slots, gathered, neighbour_states, all_stats, finished)
    return (layer_output, neighbour_gradient)


def solution(mesh):
    placed = (
        P("seq", FEATS),
        P(None, "seq", None, FEATS),
        P("seq", None),
        P("seq", None),
        P(FEATS, None),
        P("seq", FEATS),
    )
    return jax.shard_map(
        local,
        mesh=mesh,
        in_specs=placed,
        out_specs=(P("seq", FEATS), P(None, "seq", None, FEATS)),
        check_vma=False,
    )
```

```python
import functools

import jax
import jax.numpy as jnp
from jax import lax
from jax.experimental import pallas as pl
from jax.experimental.pallas import tpu as pltpu
from jax.sharding import PartitionSpec as P

HDIM = 128
SPAN = 64
NTOK = 128
KNB = 2
CAP = 2
FEATS = ("grp", "tp")
LOG2E = 1.4426950408889634
NT = (((1,), (1,)), ((), ()))
NN = (((1,), (0,)), ((), ()))
TN = (((0,), (0,)), ((), ()))
VMEM = pl.BlockSpec(memory_space=pltpu.VMEM)
SMEM = pl.BlockSpec(memory_space=pltpu.SMEM)
ANY = pl.BlockSpec(memory_space=pl.ANY)
LIMIT = pltpu.CompilerParams(vmem_limit_bytes=48 * 1024 * 1024)


def cost(gigaflops):
    return pl.CostEstimate(flops=int(gigaflops * 1e9), bytes_accessed=8 * 1024 * 1024, transcendentals=0)


def dot(a, b, dims):
    return lax.dot_general(a, b, dims, preferred_element_type=jnp.float32)


def tied(value, *others):
    return pl.pallas_call(
        lambda *refs: None,
        out_shape=jax.ShapeDtypeStruct(value.shape, value.dtype),
        in_specs=[ANY] * (1 + len(others)),
        out_specs=ANY,
        input_output_aliases={0: 0},
    )(value, *others)


def decode_slot(code):
    return code & 127, (code >> 7) & 7, code >> 10


def span_tokens(window, span, spans):
    place = lax.broadcasted_iota(jnp.int32, (16, window.shape[1]), 0)
    first_token = (place == 15) & (span < spans - 1)
    tail = jnp.where(first_token, window[:16, :], window[SPAN:, :])
    return jnp.concatenate([window[16:SPAN, :], tail], 0)


def diagonal(first, second):
    zero = jnp.zeros_like(first)
    return jnp.concatenate(
        [jnp.concatenate([first, zero], 1), jnp.concatenate([zero, second], 1)], 0
    )


def span_forward(codes, queries, cotangents, store, upper, lower, stats, held, sems):
    blocks, width = queries.shape[0] // SPAN, queries.shape[1]
    windows = blocks + 1
    heads = range(0, width, HDIM)
    scale = HDIM ** (-0.5)
    copies = []
    for i in range(KNB * windows):
        row = codes[i] & 127
        source = store.at[lax.div(row, store.shape[2]), :, lax.rem(row, store.shape[2])]
        copies.append(pltpu.make_async_copy(source, held.at[i], sems.at[i]))
        copies[-1].start()

    lane = lax.broadcasted_iota(jnp.int32, (1, 2 * SPAN), 1)
    early = lane < SPAN
    place = lax.broadcasted_iota(jnp.int32, (16, width), 0)

    def window(ref, i):
        if i == 0 or i == blocks:
            at = min(i, blocks - 1) * SPAN
            return ref[at : at + SPAN, :]
        at = i * SPAN
        tail = jnp.where(place == 15, ref[at - 16 : at, :], ref[at + SPAN - 16 : at + SPAN, :])
        return jnp.concatenate([ref[at : at + SPAN - 16, :], tail], 0)

    attended, lines = {}, {}
    for first in range(0, windows, 2):
        second = min(first + 1, windows - 1)
        for i in range(KNB * first, KNB * (second + 1)):
            copies[i].wait()
        tokens = [window(queries, i) for i in (first, second)]
        others = [window(cotangents, i) for i in (first, second)]
        live = [jnp.where(early, codes[KNB * first + k] >> 7, codes[KNB * second + k] >> 7) > 0 for k in range(KNB)]
        for h, at in enumerate(heads):
            q = diagonal(*[each[:, at : at + HDIM] for each in tokens])
            g = diagonal(*[each[:, at : at + HDIM] for each in others])
            k, v = [
                jnp.concatenate(
                    [
                        jnp.concatenate([held[KNB * i + n, kind, :, at : at + HDIM] for n in range(KNB)], 0)
                        for i in (first, second)
                    ],
                    1,
                )
                for kind in range(2)
            ]
            scores = dot(k, q, NT)
            scores = [jnp.where(live[n], scores[n * NTOK : (n + 1) * NTOK], -1e30) for n in range(KNB)]
            top = jnp.max(jnp.maximum(scores[0], scores[1]), axis=0, keepdims=True)
            weights = [
                jnp.where(live[n], jnp.exp2((scores[n] - top) * (scale * LOG2E)), 0.0) for n in range(KNB)
            ]
            total = jnp.maximum(jnp.sum(weights[0] + weights[1], axis=0, keepdims=True), 1.0)
            weights = jnp.concatenate(weights, 0) * (1.0 / total)
            delta = jnp.sum(weights * dot(v, g, NT), axis=0, keepdims=True)
            mixed = dot(weights.astype(jnp.bfloat16), v, TN)
            attended[first, h], attended[second, h] = mixed[:SPAN, :HDIM], mixed[SPAN:, HDIM:]
            lines[first, h] = jnp.concatenate([top * scale + jnp.log(total), delta], 0)

    final_row = lax.broadcasted_iota(jnp.int32, (SPAN, width), 0) == SPAN - 1
    rolled = {key: pltpu.roll(jnp.concatenate([value] * 4, 0), SPAN, 1)[:2] for key, value in lines.items()}
    for i in range(blocks):
        mixed = [jnp.concatenate([attended[j, h] for h in range(len(heads))], 1) for j in (i, i + 1)]
        half, at = (upper, i) if i < blocks // 2 else (lower, i - blocks // 2)
        half[pl.ds(at * SPAN, SPAN), :] = jnp.where(final_row, mixed[1], mixed[0]).astype(half.dtype)
        rows = []
        for h in range(len(heads)):
            both = []
            for j in (i, i + 1):
                pair = (lines[j - j % 2, h], rolled[j - j % 2, h])
                both.append(jnp.where(early, pair[j % 2], pair[1 - j % 2]))
            rows.append(jnp.where(lane % SPAN == SPAN - 1, both[1], both[0]))
        both = jnp.concatenate([row[kind : kind + 1] for kind in range(2) for row in rows], 0)
        if i % 2:
            stats[i // 2] = jnp.where(early, previous, both)
        previous = both


def pair_backward(together, slots, rows, states, stats, *rest):
    out, total, windows, sems = rest[-4:]
    spans = 2 * stats.shape[0]
    reach = SPAN + 16
    copies = []
    for i in range(slots.shape[0]):
        span = decode_slot(slots[i])[0]
        start = jnp.minimum(span * SPAN + SPAN - 16, rows.shape[0] - reach)
        source = rows.at[pl.ds(pl.multiple_of(start, 16), reach)]
        copies.append(pltpu.make_async_copy(source, windows.at[i], sems.at[i]))
        copies[-1].start()
    total[...] = jnp.zeros_like(total)
    width = states.shape[3]
    heads = width // HDIM
    scale = HDIM ** (-0.5)
    lane = lax.broadcasted_iota(jnp.int32, (1, 2 * SPAN), 1)
    early = lane < SPAN
    first_token = lane % SPAN == SPAN - 1
    last_span = spans - 1

    def block_lines(block):
        held = stats[block >> 1]
        turned = pltpu.roll(jnp.concatenate([held, held], 0), SPAN, 1)[: held.shape[0]]
        return jnp.where(early == ((block & 1) == 0), held, turned)

    def one_target(target):
        span_0, row_0, live_0 = decode_slot(slots[target * CAP])
        span_1, row_1, live_1 = decode_slot(slots[target * CAP + 1])
        tokens_0 = span_tokens(windows.at[target * CAP], span_0, spans)
        tokens_1 = span_tokens(windows.at[target * CAP + 1], span_1, spans)
        span = jnp.where(early, span_0, span_1)
        seen = (jnp.where(early, live_0, live_1) > 0) & (first_token | (span < last_span))
        lines = jnp.where(
            first_token,
            jnp.where(early, block_lines(span_0), block_lines(span_1)),
            jnp.where(
                early,
                block_lines(jnp.minimum(span_0 + 1, last_span)),
                block_lines(jnp.minimum(span_1 + 1, last_span)),
            ),
        )
        parts = []
        for h in range(heads):
            at = h * HDIM
            q = diagonal(tokens_0[:, at : at + HDIM], tokens_1[:, at : at + HDIM])
            g = diagonal(
                tokens_0[:, width + at : width + at + HDIM], tokens_1[:, width + at : width + at + HDIM]
            )
            k = jnp.concatenate([states[0, row_0, :, at : at + HDIM], states[0, row_1, :, at : at + HDIM]], 1)
            v = jnp.concatenate([states[1, row_0, :, at : at + HDIM], states[1, row_1, :, at : at + HDIM]], 1)
            both = dot(jnp.concatenate([k, v], 0), jnp.concatenate([q, g], 0), NT)
            scores = both[:NTOK, : 2 * SPAN] * scale
            weights = jnp.where(seen, jnp.exp(scores - lines[h : h + 1]), 0.0)
            grads = weights * (both[NTOK:, 2 * SPAN :] - lines[heads + h : heads + h + 1])
            key_part = dot(grads.astype(jnp.bfloat16), q, NN) * scale
            value_part = dot(weights.astype(jnp.bfloat16), g, NN)
            parts.append((key_part, value_part))
        return row_0, row_1, parts

    def some_targets(step, carry):
        for i in range(together * CAP):
            at = step * together * CAP + i
            pltpu.make_async_copy(rows.at[pl.ds(0, reach)], windows.at[at], sems.at[at]).wait()
        results = [one_target(step * together + i) for i in range(together)]
        for row_0, row_1, parts in results:
            for h, pair in enumerate(parts):
                for kind, part in enumerate(pair):
                    total[kind, row_0, :, h * HDIM : (h + 1) * HDIM] += part[:, :HDIM]
                    total[kind, row_1, :, h * HDIM : (h + 1) * HDIM] += part[:, HDIM:]
        return carry

    lax.fori_loop(0, slots.shape[0] // CAP // together, some_targets, 0)
    out[...] = total[...].astype(out.dtype)


def cut_weight(core, columns, block):
    count, _, half = block.shape
    for i in range(count):
        at = pl.multiple_of((2 * i + core[0]) * half, 128)
        block[i] = columns[:, pl.ds(at, half)]


def shifted(value, axis, steps):
    count = lax.axis_size(axis)
    return lax.ppermute(value, axis, [(source, (source + steps) % count) for source in range(count)])


def halves_round(first, second, axis):
    half = first.shape[1] // 2
    return [shifted(first[:, :half], axis, 1), shifted(second[:, half:], axis, lax.axis_size(axis) - 1)]


def source_of(steps_grp, steps_tp):
    grps, tps = lax.axis_size("grp"), lax.axis_size("tp")
    grp = lax.rem(lax.axis_index("grp") + (grps - steps_grp) % grps, grps)
    return grp * tps + lax.rem(lax.axis_index("tp") + (tps - steps_tp) % tps, tps)


def project_near(*refs):
    blocks, weights, out = refs[:6], refs[6:8], refs[-1]
    side = lax.axis_size("tp")
    rows, width = blocks[0].shape[0], weights[0].shape[1]
    for half in range(2):
        for kind, weight in enumerate(weights):
            total = None
            for block, step in zip(blocks[half * 3 : half * 3 + 3], (0, 1, side - 1)):
                for inner in range(side):
                    source = source_of(inner, step) if half == 0 else source_of(step, inner)
                    term = dot(block[:, inner * width : (inner + 1) * width], weight[source], NN)
                    total = term if total is None else total + term
            out[kind, pl.ds(half * rows, rows), :] = total


def project_far(*refs):
    blocks, weights, partial, out, finished = refs[:4], refs[4:6], refs[6], refs[7], refs[8]
    finished[...] = jnp.zeros_like(finished)
    side = lax.axis_size("tp")
    rows, width = blocks[0].shape[0], weights[0].shape[1]
    columns = weights[0].shape[2]
    core = lax.rem(lax.axis_index("seq"), 2)
    for half in range(2):
        for kind, weight in enumerate(weights):
            total = partial[kind, pl.ds(half * rows, rows), :]
            for inner in range(side):
                block = blocks[half * 2 + inner // (side // 2)]
                at = inner % (side // 2) * width
                far = side // 2
                source = source_of(inner, far) if half == 0 else source_of(far, inner)
                total = total + dot(block[:, at : at + width], weight[source], NN)
            at = pl.multiple_of((core if kind == 0 else 1 - core) * columns, 128)
            out[pl.ds(half * rows, rows), pl.ds(at, columns)] = total.astype(out.dtype)


def local(queries, neighbour_states, retrieved, valid_blocks, output_weight, attention_cotangent):
    owners = lax.axis_size("seq")
    grps, tps = lax.axis_size("grp"), lax.axis_size("tp")
    me = lax.axis_index("seq")
    tok_rows, width = queries.shape
    span_count = tok_rows // SPAN
    request_count = span_count * KNB
    store_rows = neighbour_states.shape[1]
    out_columns = output_weight.shape[1] // (grps * tps)

    core = (me & 1).reshape(1)
    half = out_columns // 2
    sources = 4 if grps * tps % 4 == 0 else 1
    cut = pl.pallas_call(
        cut_weight,
        grid_spec=pltpu.PrefetchScalarGridSpec(
            num_scalar_prefetch=1,
            grid=(grps * tps // sources,),
            in_specs=[pl.BlockSpec((width, sources * out_columns), lambda i, core: (0, i))],
            out_specs=pl.BlockSpec((sources, width, half), lambda i, core: (i, 0, 0)),
        ),
        out_shape=jax.ShapeDtypeStruct((grps * tps, width, half), jnp.bfloat16),
    )(core, output_weight)
    weight = lax.all_to_all(cut, FEATS, split_axis=0, concat_axis=0, tiled=True)

    table = lax.all_gather(
        jnp.stack([retrieved.reshape(request_count), valid_blocks.reshape(request_count)]), "seq", axis=0
    )
    owner_of = table[:, 0] // store_rows
    same_owner = owner_of[:, :, None] == owner_of[:, None, :]
    order = jnp.arange(request_count, dtype=jnp.int32)
    earlier = order[None, :] < order[:, None]
    position = jnp.sum((same_owner & earlier[None]).astype(jnp.int32), axis=2)
    span_of = jnp.arange(owners, dtype=jnp.int32)[:, None] * span_count + order[None, :] // KNB
    code = span_of + 128 * (table[:, 0] % store_rows) + 1024 * (table[:, 1] > 0).astype(jnp.int32)
    hit = (owner_of == me)[:, None, :] & (
        position[:, None, :] == jnp.arange(CAP, dtype=jnp.int32)[None, :, None]
    )
    slots = jnp.sum(jnp.where(hit, code[:, None, :], 0), axis=2).reshape(owners * CAP)
    plain = (table[:, 0] + 128 * (table[:, 1] > 0).astype(jnp.int32)).reshape(owners * request_count)
    plain = jnp.concatenate([jnp.zeros((KNB,), jnp.int32), plain])
    codes = lax.dynamic_slice_in_dim(plain, me * request_count, request_count + KNB, 0)

    store = lax.all_gather(neighbour_states, "seq", axis=0)
    store = tied(store, slots, codes, weight)
    both = tied(jnp.concatenate([queries, attention_cotangent], axis=1), weight)
    gathered = lax.all_gather(both, "seq", axis=0, tiled=True)
    weight_other = lax.ppermute(weight, "seq", [(source, source ^ 1) for source in range(owners)])

    middle = tok_rows // 2
    upper, lower, stats = pl.pallas_call(
        span_forward,
        cost_estimate=cost(5),
        out_shape=(
            jax.ShapeDtypeStruct((middle, width), jnp.bfloat16),
            jax.ShapeDtypeStruct((middle, width), jnp.bfloat16),
            jax.ShapeDtypeStruct((span_count // 2, 2 * width // HDIM, 2 * SPAN), jnp.float32),
        ),
        in_specs=[SMEM, VMEM, VMEM, ANY],
        out_specs=(VMEM, VMEM, VMEM),
        scratch_shapes=[
            pltpu.VMEM((request_count + KNB, 2, NTOK, width), jnp.bfloat16),
            pltpu.SemaphoreType.DMA((request_count + KNB,)),
        ],
        compiler_params=LIMIT,
    )(codes, queries, attention_cotangent, store)

    lower = jnp.concatenate([lower] + [shifted(lower, "tp", i) for i in range(1, tps)], 1)
    upper = jnp.concatenate([upper] + [shifted(upper, "grp", i) for i in range(1, grps)], 1)
    upper = [upper, shifted(upper, "tp", 1), shifted(upper, "tp", tps - 1)]
    lower = [lower, shifted(lower, "grp", 1), shifted(lower, "grp", grps - 1)]
    far = halves_round(upper[1], upper[2], "tp") + halves_round(lower[1], lower[2], "grp")
    total = pl.pallas_call(
        project_near,
        cost_estimate=cost(3),
        out_shape=jax.ShapeDtypeStruct((2, tok_rows, half), jnp.float32),
        in_specs=[VMEM] * 8,
        out_specs=VMEM,
        compiler_params=LIMIT,
    )(*upper, *lower, weight, weight_other)
    layer_output, finished = pl.pallas_call(
        project_far,
        cost_estimate=cost(2),
        out_shape=(
            jax.ShapeDtypeStruct((tok_rows, out_columns), jnp.bfloat16),
            jax.ShapeDtypeStruct((8, HDIM), jnp.float32),
        ),
        in_specs=[VMEM] * 7,
        out_specs=(VMEM, VMEM),
        compiler_params=LIMIT,
    )(*far, weight, weight_other, total)

    all_stats = lax.all_to_all(
        jnp.broadcast_to(stats[None], (owners, *stats.shape)), "seq", split_axis=0, concat_axis=0, tiled=True
    ).reshape(owners * span_count // 2, *stats.shape[1:])
    neighbour_gradient = pl.pallas_call(
        functools.partial(pair_backward, 8),
        cost_estimate=cost(10),
        out_shape=jax.ShapeDtypeStruct(neighbour_states.shape, jnp.bfloat16),
        in_specs=[SMEM, ANY, VMEM, VMEM, VMEM],
        out_specs=VMEM,
        scratch_shapes=[
            pltpu.VMEM(neighbour_states.shape, jnp.float32),
            pltpu.VMEM((owners * CAP, SPAN + 16, 2 * width), jnp.bfloat16),
            pltpu.SemaphoreType.DMA((owners * CAP,)),
        ],
        compiler_params=LIMIT,
    )(slots, gathered, neighbour_states, all_stats, finished)
    return (layer_output, neighbour_gradient)


def solution(mesh):
    placed = (
        P("seq", FEATS),
        P(None, "seq", None, FEATS),
        P("seq", None),
        P("seq", None),
        P(FEATS, None),
        P("seq", FEATS),
    )
    return jax.shard_map(
        local,
        mesh=mesh,
        in_specs=placed,
        out_specs=(P("seq", FEATS), P(None, "seq", None, FEATS)),
        check_vma=False,
    )
```

```python
import functools

import jax
import jax.numpy as jnp
from jax import lax
from jax.experimental import pallas as pl
from jax.experimental.pallas import tpu as pltpu
from jax.sharding import PartitionSpec as P

HDIM = 128
SPAN = 64
NTOK = 128
KNB = 2
CAP = 2
FEATS = ("grp", "tp")
LOG2E = 1.4426950408889634
NT = (((1,), (1,)), ((), ()))
NN = (((1,), (0,)), ((), ()))
TN = (((0,), (0,)), ((), ()))
VMEM = pl.BlockSpec(memory_space=pltpu.VMEM)
SMEM = pl.BlockSpec(memory_space=pltpu.SMEM)
ANY = pl.BlockSpec(memory_space=pl.ANY)
LIMIT = pltpu.CompilerParams(vmem_limit_bytes=48 * 1024 * 1024)


def cost(gigaflops):
    return pl.CostEstimate(flops=int(gigaflops * 1e9), bytes_accessed=8 * 1024 * 1024, transcendentals=0)


def dot(a, b, dims):
    return lax.dot_general(a, b, dims, preferred_element_type=jnp.float32)


def tied(value, *others):
    return pl.pallas_call(
        lambda *refs: None,
        out_shape=jax.ShapeDtypeStruct(value.shape, value.dtype),
        in_specs=[ANY] * (1 + len(others)),
        out_specs=ANY,
        input_output_aliases={0: 0},
    )(value, *others)


def decode_slot(code):
    return code & 127, (code >> 7) & 7, code >> 10


def span_tokens(window, span, spans):
    place = lax.broadcasted_iota(jnp.int32, (16, window.shape[1]), 0)
    first_token = (place == 15) & (span < spans - 1)
    tail = jnp.where(first_token, window[:16, :], window[SPAN:, :])
    return jnp.concatenate([window[16:SPAN, :], tail], 0)


def diagonal(first, second):
    zero = jnp.zeros_like(first)
    return jnp.concatenate(
        [jnp.concatenate([first, zero], 1), jnp.concatenate([zero, second], 1)], 0
    )


def span_forward(codes, queries, cotangents, store, upper, lower, stats, held, sems):
    blocks, width = queries.shape[0] // SPAN, queries.shape[1]
    windows = blocks + 1
    heads = range(0, width, HDIM)
    scale = HDIM ** (-0.5)
    copies = []
    for i in range(KNB * windows):
        row = codes[i] & 127
        source = store.at[lax.div(row, store.shape[2]), :, lax.rem(row, store.shape[2])]
        copies.append(pltpu.make_async_copy(source, held.at[i], sems.at[i]))
        copies[-1].start()

    lane = lax.broadcasted_iota(jnp.int32, (1, 2 * SPAN), 1)
    early = lane < SPAN
    place = lax.broadcasted_iota(jnp.int32, (16, width), 0)

    def window(ref, i):
        if i == 0 or i == blocks:
            at = min(i, blocks - 1) * SPAN
            return ref[at : at + SPAN, :]
        at = i * SPAN
        tail = jnp.where(place == 15, ref[at - 16 : at, :], ref[at + SPAN - 16 : at + SPAN, :])
        return jnp.concatenate([ref[at : at + SPAN - 16, :], tail], 0)

    attended, lines = {}, {}
    for first in range(0, windows, 2):
        second = min(first + 1, windows - 1)
        for i in range(KNB * first, KNB * (second + 1)):
            copies[i].wait()
        tokens = [window(queries, i) for i in (first, second)]
        others = [window(cotangents, i) for i in (first, second)]
        live = [jnp.where(early, codes[KNB * first + k] >> 7, codes[KNB * second + k] >> 7) > 0 for k in range(KNB)]
        for h, at in enumerate(heads):
            q = diagonal(*[each[:, at : at + HDIM] for each in tokens])
            g = diagonal(*[each[:, at : at + HDIM] for each in others])
            k, v = [
                jnp.concatenate(
                    [
                        jnp.concatenate([held[KNB * i + n, kind, :, at : at + HDIM] for n in range(KNB)], 0)
                        for i in (first, second)
                    ],
                    1,
                )
                for kind in range(2)
            ]
            scores = dot(k, q, NT)
            scores = [jnp.where(live[n], scores[n * NTOK : (n + 1) * NTOK], -1e30) for n in range(KNB)]
            top = jnp.max(jnp.maximum(scores[0], scores[1]), axis=0, keepdims=True)
            weights = [
                jnp.where(live[n], jnp.exp2((scores[n] - top) * (scale * LOG2E)), 0.0) for n in range(KNB)
            ]
            total = jnp.maximum(jnp.sum(weights[0] + weights[1], axis=0, keepdims=True), 1.0)
            weights = jnp.concatenate(weights, 0) * (1.0 / total)
            delta = jnp.sum(weights * dot(v, g, NT), axis=0, keepdims=True)
            mixed = dot(weights.astype(jnp.bfloat16), v, TN)
            attended[first, h], attended[second, h] = mixed[:SPAN, :HDIM], mixed[SPAN:, HDIM:]
            lines[first, h] = jnp.concatenate([top * scale + jnp.log(total), delta], 0)

    final_row = lax.broadcasted_iota(jnp.int32, (SPAN, width), 0) == SPAN - 1
    rolled = {key: pltpu.roll(jnp.concatenate([value] * 4, 0), SPAN, 1)[:2] for key, value in lines.items()}
    for i in range(blocks):
        mixed = [jnp.concatenate([attended[j, h] for h in range(len(heads))], 1) for j in (i, i + 1)]
        half, at = (upper, i) if i < blocks // 2 else (lower, i - blocks // 2)
        half[pl.ds(at * SPAN, SPAN), :] = jnp.where(final_row, mixed[1], mixed[0]).astype(half.dtype)
        rows = []
        for h in range(len(heads)):
            both = []
            for j in (i, i + 1):
                pair = (lines[j - j % 2, h], rolled[j - j % 2, h])
                both.append(jnp.where(early, pair[j % 2], pair[1 - j % 2]))
            rows.append(jnp.where(lane % SPAN == SPAN - 1, both[1], both[0]))
        both = jnp.concatenate([row[kind : kind + 1] for kind in range(2) for row in rows], 0)
        if i % 2:
            stats[i // 2] = jnp.where(early, previous, both)
        previous = both


def pair_backward(together, slots, rows, states, stats, *rest):
    out, total, windows, sems = rest[-4:]
    spans = 2 * stats.shape[0]
    reach = SPAN + 16
    copies = []
    for i in range(slots.shape[0]):
        span = decode_slot(slots[i])[0]
        start = jnp.minimum(span * SPAN + SPAN - 16, rows.shape[0] - reach)
        source = rows.at[pl.ds(pl.multiple_of(start, 16), reach)]
        copies.append(pltpu.make_async_copy(source, windows.at[i], sems.at[i]))
        copies[-1].start()
    total[...] = jnp.zeros_like(total)
    width = states.shape[3]
    heads = width // HDIM
    scale = HDIM ** (-0.5)
    lane = lax.broadcasted_iota(jnp.int32, (1, 2 * SPAN), 1)
    early = lane < SPAN
    first_token = lane % SPAN == SPAN - 1
    last_span = spans - 1

    def block_lines(block):
        held = stats[block >> 1]
        turned = pltpu.roll(jnp.concatenate([held, held], 0), SPAN, 1)[: held.shape[0]]
        return jnp.where(early == ((block & 1) == 0), held, turned)

    def one_target(target):
        span_0, row_0, live_0 = decode_slot(slots[target * CAP])
        span_1, row_1, live_1 = decode_slot(slots[target * CAP + 1])
        tokens_0 = span_tokens(windows.at[target * CAP], span_0, spans)
        tokens_1 = span_tokens(windows.at[target * CAP + 1], span_1, spans)
        span = jnp.where(early, span_0, span_1)
        seen = (jnp.where(early, live_0, live_1) > 0) & (first_token | (span < last_span))
        lines = jnp.where(
            first_token,
            jnp.where(early, block_lines(span_0), block_lines(span_1)),
            jnp.where(
                early,
                block_lines(jnp.minimum(span_0 + 1, last_span)),
                block_lines(jnp.minimum(span_1 + 1, last_span)),
            ),
        )
        parts = []
        for h in range(heads):
            at = h * HDIM
            q = diagonal(tokens_0[:, at : at + HDIM], tokens_1[:, at : at + HDIM])
            g = diagonal(
                tokens_0[:, width + at : width + at + HDIM], tokens_1[:, width + at : width + at + HDIM]
            )
            k = jnp.concatenate([states[0, row_0, :, at : at + HDIM], states[0, row_1, :, at : at + HDIM]], 1)
            v = jnp.concatenate([states[1, row_0, :, at : at + HDIM], states[1, row_1, :, at : at + HDIM]], 1)
            both = dot(jnp.concatenate([k, v], 0), jnp.concatenate([q, g], 0), NT)
            scores = both[:NTOK, : 2 * SPAN] * scale
            weights = jnp.where(seen, jnp.exp(scores - lines[h : h + 1]), 0.0)
            grads = weights * (both[NTOK:, 2 * SPAN :] - lines[heads + h : heads + h + 1])
            key_part = dot(grads.astype(jnp.bfloat16), q, NN) * scale
            value_part = dot(weights.astype(jnp.bfloat16), g, NN)
            parts.append((key_part, value_part))
        return row_0, row_1, parts

    def some_targets(step, carry):
        for i in range(together * CAP):
            at = step * together * CAP + i
            pltpu.make_async_copy(rows.at[pl.ds(0, reach)], windows.at[at], sems.at[at]).wait()
        results = [one_target(step * together + i) for i in range(together)]
        for row_0, row_1, parts in results:
            for h, pair in enumerate(parts):
                for kind, part in enumerate(pair):
                    total[kind, row_0, :, h * HDIM : (h + 1) * HDIM] += part[:, :HDIM]
                    total[kind, row_1, :, h * HDIM : (h + 1) * HDIM] += part[:, HDIM:]
        return carry

    lax.fori_loop(0, slots.shape[0] // CAP // together, some_targets, 0)
    out[...] = total[...].astype(out.dtype)


def cut_weight(core, columns, block):
    count, _, half = block.shape
    for i in range(count):
        at = pl.multiple_of((2 * i + core[0]) * half, 128)
        block[i] = columns[:, pl.ds(at, half)]


def shifted(value, axis, steps):
    count = lax.axis_size(axis)
    return lax.ppermute(value, axis, [(source, (source + steps) % count) for source in range(count)])


def halves_round(first, second, axis):
    half = first.shape[1] // 2
    return [shifted(first[:, :half], axis, 1), shifted(second[:, half:], axis, lax.axis_size(axis) - 1)]


def source_of(steps_grp, steps_tp):
    grps, tps = lax.axis_size("grp"), lax.axis_size("tp")
    grp = lax.rem(lax.axis_index("grp") + (grps - steps_grp) % grps, grps)
    return grp * tps + lax.rem(lax.axis_index("tp") + (tps - steps_tp) % tps, tps)


def project_near(*refs):
    blocks, weights, out = refs[:6], refs[6:8], refs[-1]
    side = lax.axis_size("tp")
    rows, width = blocks[0].shape[0], weights[0].shape[1]
    for half in range(2):
        for kind, weight in enumerate(weights):
            total = None
            for block, step in zip(blocks[half * 3 : half * 3 + 3], (0, 1, side - 1)):
                for inner in range(side):
                    source = source_of(inner, step) if half == 0 else source_of(step, inner)
                    term = dot(block[:, inner * width : (inner + 1) * width], weight[source], NN)
                    total = term if total is None else total + term
            out[kind, pl.ds(half * rows, rows), :] = total


def project_far(*refs):
    blocks, weights, partial, out, finished = refs[:4], refs[4:6], refs[6], refs[7], refs[8]
    finished[...] = jnp.zeros_like(finished)
    side = lax.axis_size("tp")
    rows, width = blocks[0].shape[0], weights[0].shape[1]
    columns = weights[0].shape[2]
    core = lax.rem(lax.axis_index("seq"), 2)
    for half in range(2):
        for kind, weight in enumerate(weights):
            total = partial[kind, pl.ds(half * rows, rows), :]
            for inner in range(side):
                block = blocks[half * 2 + inner // (side // 2)]
                at = inner % (side // 2) * width
                far = side // 2
                source = source_of(inner, far) if half == 0 else source_of(far, inner)
                total = total + dot(block[:, at : at + width], weight[source], NN)
            at = pl.multiple_of((core if kind == 0 else 1 - core) * columns, 128)
            out[pl.ds(half * rows, rows), pl.ds(at, columns)] = total.astype(out.dtype)


def local(queries, neighbour_states, retrieved, valid_blocks, output_weight, attention_cotangent):
    owners = lax.axis_size("seq")
    grps, tps = lax.axis_size("grp"), lax.axis_size("tp")
    me = lax.axis_index("seq")
    tok_rows, width = queries.shape
    span_count = tok_rows // SPAN
    request_count = span_count * KNB
    store_rows = neighbour_states.shape[1]
    out_columns = output_weight.shape[1] // (grps * tps)

    core = (me & 1).reshape(1)
    half = out_columns // 2
    sources = 4 if grps * tps % 4 == 0 else 1
    cut = pl.pallas_call(
        cut_weight,
        grid_spec=pltpu.PrefetchScalarGridSpec(
            num_scalar_prefetch=1,
            grid=(grps * tps // sources,),
            in_specs=[pl.BlockSpec((width, sources * out_columns), lambda i, core: (0, i))],
            out_specs=pl.BlockSpec((sources, width, half), lambda i, core: (i, 0, 0)),
        ),
        out_shape=jax.ShapeDtypeStruct((grps * tps, width, half), jnp.bfloat16),
    )(core, output_weight)
    weight = lax.all_to_all(cut, FEATS, split_axis=0, concat_axis=0, tiled=True)

    table = lax.all_gather(
        jnp.stack([retrieved.reshape(request_count), valid_blocks.reshape(request_count)]), "seq", axis=0
    )
    owner_of = table[:, 0] // store_rows
    same_owner = owner_of[:, :, None] == owner_of[:, None, :]
    order = jnp.arange(request_count, dtype=jnp.int32)
    earlier = order[None, :] < order[:, None]
    position = jnp.sum((same_owner & earlier[None]).astype(jnp.int32), axis=2)
    span_of = jnp.arange(owners, dtype=jnp.int32)[:, None] * span_count + order[None, :] // KNB
    code = span_of + 128 * (table[:, 0] % store_rows) + 1024 * (table[:, 1] > 0).astype(jnp.int32)
    hit = (owner_of == me)[:, None, :] & (
        position[:, None, :] == jnp.arange(CAP, dtype=jnp.int32)[None, :, None]
    )
    slots = jnp.sum(jnp.where(hit, code[:, None, :], 0), axis=2).reshape(owners * CAP)
    plain = (table[:, 0] + 128 * (table[:, 1] > 0).astype(jnp.int32)).reshape(owners * request_count)
    plain = jnp.concatenate([jnp.zeros((KNB,), jnp.int32), plain])
    codes = lax.dynamic_slice_in_dim(plain, me * request_count, request_count + KNB, 0)

    store = lax.all_gather(neighbour_states, "seq", axis=0)
    store = tied(store, slots, weight)
    both = tied(jnp.concatenate([queries, attention_cotangent], axis=1), weight)
    gathered = lax.all_gather(both, "seq", axis=0, tiled=True)
    weight_other = lax.ppermute(weight, "seq", [(source, source ^ 1) for source in range(owners)])

    middle = tok_rows // 2
    upper, lower, stats = pl.pallas_call(
        span_forward,
        cost_estimate=cost(5),
        out_shape=(
            jax.ShapeDtypeStruct((middle, width), jnp.bfloat16),
            jax.ShapeDtypeStruct((middle, width), jnp.bfloat16),
            jax.ShapeDtypeStruct((span_count // 2, 2 * width // HDIM, 2 * SPAN), jnp.float32),
        ),
        in_specs=[SMEM, VMEM, VMEM, ANY],
        out_specs=(VMEM, VMEM, VMEM),
        scratch_shapes=[
            pltpu.VMEM((request_count + KNB, 2, NTOK, width), jnp.bfloat16),
            pltpu.SemaphoreType.DMA((request_count + KNB,)),
        ],
        compiler_params=LIMIT,
    )(codes, queries, attention_cotangent, store)

    lower = jnp.concatenate([lower] + [shifted(lower, "tp", i) for i in range(1, tps)], 1)
    upper = jnp.concatenate([upper] + [shifted(upper, "grp", i) for i in range(1, grps)], 1)
    upper = [upper, shifted(upper, "tp", 1), shifted(upper, "tp", tps - 1)]
    lower = [lower, shifted(lower, "grp", 1), shifted(lower, "grp", grps - 1)]
    far = halves_round(upper[1], upper[2], "tp") + halves_round(lower[1], lower[2], "grp")
    total = pl.pallas_call(
        project_near,
        cost_estimate=cost(3),
        out_shape=jax.ShapeDtypeStruct((2, tok_rows, half), jnp.float32),
        in_specs=[VMEM] * 8,
        out_specs=VMEM,
        compiler_params=LIMIT,
    )(*upper, *lower, weight, weight_other)
    layer_output, finished = pl.pallas_call(
        project_far,
        cost_estimate=cost(2),
        out_shape=(
            jax.ShapeDtypeStruct((tok_rows, out_columns), jnp.bfloat16),
            jax.ShapeDtypeStruct((8, HDIM), jnp.float32),
        ),
        in_specs=[VMEM] * 7,
        out_specs=(VMEM, VMEM),
        compiler_params=LIMIT,
    )(*far, weight, weight_other, total)

    all_stats = lax.all_to_all(
        jnp.broadcast_to(stats[None], (owners, *stats.shape)), "seq", split_axis=0, concat_axis=0, tiled=True
    ).reshape(owners * span_count // 2, *stats.shape[1:])
    neighbour_gradient = pl.pallas_call(
        functools.partial(pair_backward, 8),
        cost_estimate=cost(10),
        out_shape=jax.ShapeDtypeStruct(neighbour_states.shape, jnp.bfloat16),
        in_specs=[SMEM, ANY, VMEM, VMEM, VMEM],
        out_specs=VMEM,
        scratch_shapes=[
            pltpu.VMEM(neighbour_states.shape, jnp.float32),
            pltpu.VMEM((owners * CAP, SPAN + 16, 2 * width), jnp.bfloat16),
            pltpu.SemaphoreType.DMA((owners * CAP,)),
        ],
        compiler_params=LIMIT,
    )(slots, gathered, neighbour_states, all_stats, finished)
    return (layer_output, neighbour_gradient)


def solution(mesh):
    placed = (
        P("seq", FEATS),
        P(None, "seq", None, FEATS),
        P("seq", None),
        P("seq", None),
        P(FEATS, None),
        P("seq", FEATS),
    )
    return jax.shard_map(
        local,
        mesh=mesh,
        in_specs=placed,
        out_specs=(P("seq", FEATS), P(None, "seq", None, FEATS)),
        check_vma=False,
    )
```
